32 devices in a mesh: depth: 4 (over y, core), freq: 8 (over z, x).
Axes of the slice: x: 2, y: 2, z: 4, core: 2. Of those that a mesh axis runs over, the one named last changes fastest.
Arguments:
- source_top: bfloat16 [2, 8, 2, 512, 512], P(None, 'freq'), may hold values from -6 to 6
- receiver_top: bfloat16 [2, 8, 2, 512, 512], P(None, 'freq'), may hold values from -6 to 6
- slowness_codes: int32 [4, 1024, 1024], P('depth'), may hold values from 0 to 31
- slowness_table: float32 [32], replicated, may hold values from 0.8 to 1.25
- anchors: int32 [2, 2], replicated, may hold values from 0 to 512, as said below
Outputs:
- image: float32 [4, 15, 512, 512], P('depth', None, 'freq')
The draws below stay inside these ranges and needn't reach their ends.
Inputs may be any that keep to these rules, and one draw needn't show every extreme that they name: `anchors`: each of the two coordinates is 0 for some shot and 512 for another.
All inputs are finite; a program needn't handle non-finite values.
Results may differ from the reference program's by a relative error of at most 0.03.
Values may be sent and summed in bfloat16 or wider, within the bound.
No kernel may reach another device: no remote copies, remote signals or barrier semaphores. Data moves between devices by JAX's collectives and lax.ppermute only.
A program may use at most 192 MiB of HBM per device.

```python
import math
import jax
import jax.numpy as jnp
from jax import lax

NX = 512
NY = 512
MX = 1024
NCODE = 32
LAG = 7
SHOTS = 2
FREQS = 8
NZ = 4


def draw_anchors(key, part):
    key_base, key_first, key_second = jax.random.split(jax.random.fold_in(key, 7), 3)
    corners = jax.random.randint(key_base, (SHOTS, 2), 0, MX - NX + 1)
    order_first = jax.random.permutation(key_first, SHOTS)
    order_second = jax.random.permutation(key_second, SHOTS)
    corners = corners.at[order_first[0], 0].set(0)
    corners = corners.at[order_first[1], 0].set(MX - NX)
    corners = corners.at[order_second[0], 1].set(0)
    corners = corners.at[order_second[1], 1].set(MX - NX)
    return corners.astype(jnp.int32)


def plant(drawn, own_key, least, top_value):
    longest = drawn.shape.index(max(drawn.shape))
    spots = []
    for shift in (0, 1):
        where = [jax.random.randint(jax.random.fold_in(own_key, axis), (), 0, length) for axis, length in enumerate(drawn.shape)]
        where[longest] = (where[longest] + shift) % drawn.shape[longest]
        spots.append(tuple(where))
    return drawn.at[spots[0]].set(least).at[spots[1]].set(top_value)


def level_of(own_key, extent, shards, least, largest):
    level, own = 1.0, jax.random.fold_in(own_key, 6)
    for dim, shards_of in shards:
        steps = jnp.exp(jax.random.uniform(jax.random.fold_in(own, dim), (shards_of,), jnp.float32, least / len(shards), largest / len(shards)))
        level = level * jnp.repeat(steps, extent[dim] // shards_of).reshape([-1 if axis == dim else 1 for axis in range(len(extent))])
    return level


def scatter_about(stream_key, extent, deviation, bound, cuts=(), kind=jnp.bfloat16):
    level = level_of(stream_key, extent, cuts, -0.22, 0.18) if cuts else 1.0
    drawn = jax.random.normal(stream_key, extent, jnp.float32) * deviation * level
    return jnp.minimum(jnp.maximum(drawn, -bound), bound).astype(kind)


def setup_inputs(seed: int = 0) -> dict:
    arg_keys = jax.random.split(jax.random.key(seed), 6)
    source_top = scatter_about(arg_keys[0], (SHOTS, FREQS, 2, NX, NY), 1.0, 6.0, ((1, 8),))
    receiver_top = scatter_about(arg_keys[1], (SHOTS, FREQS, 2, NX, NY), 1.0, 6.0, ((1, 8),))
    slowness_codes = plant(jax.random.randint(arg_keys[2], (NZ, MX, MX), 0, NCODE), jax.random.fold_in(arg_keys[2], 1), 0, NCODE - 1).astype(jnp.int32)
    slowness_table = jnp.clip(jax.random.uniform(arg_keys[3], (NCODE,), jnp.float32, 0.8, 1.25), 0.8, 1.25)
    anchors = draw_anchors(jax.random.fold_in(arg_keys[5], 71), 0)
    return dict(source_top=source_top, receiver_top=receiver_top, slowness_codes=slowness_codes, slowness_table=slowness_table, anchors=anchors)


def transform_tables(length):
    position = jnp.arange(length, dtype=jnp.int32)
    product = position[:, None] * position[None, :] % length
    angles = product.astype(jnp.float32) * (2.0 * math.pi / length)
    factor = 1.0 / math.sqrt(length)
    return (jnp.cos(angles) * factor, jnp.sin(angles) * factor)

def build_tables(len_x, len_y):
    cos_x, sin_x = transform_tables(len_x)
    cos_y, sin_y = transform_tables(len_y)
    fwd_x = jnp.stack([jnp.stack([cos_x, sin_x]), jnp.stack([-sin_x, cos_x])]).astype(jnp.bfloat16)
    inv_x = jnp.stack([jnp.stack([cos_x, -sin_x]), jnp.stack([sin_x, cos_x])]).astype(jnp.bfloat16)
    fwd_y = jnp.stack([jnp.stack([cos_y, -sin_y], axis=1), jnp.stack([sin_y, cos_y], axis=1)]).astype(jnp.bfloat16)
    inv_y = jnp.stack([jnp.stack([cos_y, sin_y], axis=1), jnp.stack([-sin_y, cos_y], axis=1)]).astype(jnp.bfloat16)
    return (fwd_x, inv_x, fwd_y, inv_y)

def wavenumbers(length):
    position = jnp.arange(length, dtype=jnp.int32)
    signed = jnp.where(position < length // 2, position, position - length)
    return signed.astype(jnp.float32) * (2.0 * math.pi / length)

def aperture_slowness(code_plane, slowness_table, corner, rows_x, rows_y):
    window = lax.dynamic_slice(code_plane, (corner[0].astype(jnp.int32), corner[1].astype(jnp.int32)), (rows_x, rows_y))
    levels = jnp.arange(slowness_table.shape[0], dtype=jnp.int32)
    return lax.optimization_barrier(jnp.sum(jnp.where(window[None] == levels[:, None, None], slowness_table[:, None, None], 0.0), axis=0))

def propagators(slowness, angular, wave_x, wave_y):
    mean_slowness = jnp.mean(slowness)
    vertical = (angular * mean_slowness) ** 2 - wave_x[:, None] ** 2 - wave_y[None, :] ** 2
    travel = jnp.sqrt(jnp.maximum(vertical, 0.0))
    damping = jnp.exp(-jnp.sqrt(jnp.maximum(-vertical, 0.0)))
    screen_angle = angular * (slowness - mean_slowness)
    return (damping * jnp.cos(travel), damping * jnp.sin(travel), jnp.cos(screen_angle), jnp.sin(screen_angle))

def advance(fields, tables, operators):
    fwd_x, inv_x, fwd_y, inv_y = tables
    conjugate = jnp.array([1.0, -1.0], jnp.float32)[None, :, None, None]
    across_x = jnp.einsum('pqxu,gfquy->gfpxy', fwd_x.astype(jnp.float32), fields.astype(jnp.float32)).astype(jnp.bfloat16)
    second = jnp.einsum('gfqxu,qupb->gfxpb', across_x.astype(jnp.float32), fwd_y.astype(jnp.float32))
    real_part = second[:, :, :, 0]
    imag_part = second[:, :, :, 1]
    phase_re = operators[0][:, None]
    phase_im = operators[1][:, None] * conjugate
    shifted = jnp.stack([real_part * phase_re - imag_part * phase_im, real_part * phase_im + imag_part * phase_re], axis=3).astype(jnp.bfloat16)
    back_y = jnp.einsum('gfxqu,qupb->gfxpb', shifted.astype(jnp.float32), inv_y.astype(jnp.float32)).astype(jnp.bfloat16)
    fourth = jnp.einsum('pqxu,gfuqy->gfpxy', inv_x.astype(jnp.float32), back_y.astype(jnp.float32))
    real_part = fourth[:, :, 0]
    imag_part = fourth[:, :, 1]
    turn_re = operators[2][:, None]
    turn_im = operators[3][:, None] * conjugate
    return jnp.stack([real_part * turn_re - imag_part * turn_im, real_part * turn_im + imag_part * turn_re], axis=2).astype(jnp.bfloat16)

def correlate(source, receiver, row_count):
    lag_terms = []
    for offset in range(-LAG, LAG + 1):
        shifted_source = source[:, :, :, LAG - offset:LAG - offset + row_count].astype(jnp.float32)
        shifted_receiver = receiver[:, :, :, LAG + offset:LAG + offset + row_count].astype(jnp.float32)
        lag_terms.append(lax.optimization_barrier(jnp.sum(shifted_source * shifted_receiver, axis=(1, 2))))
    return jnp.stack(lag_terms, axis=1)

def reference(source_top, receiver_top, slowness_codes, slowness_table, anchors):
    tables = build_tables(NX, NY)
    wave_x = wavenumbers(NX)
    wave_y = wavenumbers(NY)
    freq_total = source_top.shape[1]
    factor = 1.0 / math.sqrt(2.0 * SHOTS * freq_total)

    def one_shot(image_sum, shot_index):
        corner = anchors[shot_index]

        def one_freq(image_acc, freq_index):
            angular = math.pi * (0.45 + 0.5 * (freq_index.astype(jnp.float32) + 0.5) / freq_total)
            angular = jnp.reshape(angular, (1, 1, 1))
            fields = jnp.stack([source_top[shot_index, freq_index], receiver_top[shot_index, freq_index]])[None]

            def one_plane(current, code_plane):
                slowness = aperture_slowness(code_plane, slowness_table, corner, NX, NY)
                operators = propagators(slowness, angular, wave_x, wave_y)
                current = advance(current, tables, operators)
                padded = jnp.pad(current[0], ((0, 0), (0, 0), (LAG, LAG), (0, 0)))
                lag_image = correlate(padded[0][None, None], padded[1][None, None], NX)[0]
                return (current, lag_image)
            unused, lag_images = lax.scan(one_plane, fields, slowness_codes)
            return (image_acc + lag_images, None)
        image_sum, unused = lax.scan(one_freq, image_sum, jnp.arange(freq_total, dtype=jnp.int32))
        return (image_sum, None)
    image_sum = jnp.zeros((NZ, 2 * LAG + 1, NX, NY), jnp.float32)
    image_sum, unused = lax.scan(one_shot, image_sum, jnp.arange(SHOTS, dtype=jnp.int32))
    return image_sum * factor
```

```python
import functools
import math

import jax
import jax.numpy as jnp
import ml_dtypes
import numpy as np
from jax import lax
from jax.experimental import pallas as pl
from jax.experimental.pallas import tpu as pltpu
from jax.sharding import PartitionSpec as P

LAG = 7
HALO = 8
LANES = 128
AXES = ("depth", "freq")
VMEM_BYTES = 56 * 2**20


def parity_tables(length):
    position = np.arange(length, dtype=np.int64)
    product = position[:, None] * position[None, :] % length
    angles = product.astype(np.float32) * np.float32(2.0 * math.pi / length)
    factor = np.float32(1.0 / math.sqrt(length))
    cos, sin = np.cos(angles) * factor, np.sin(angles) * factor
    half = length // 2
    tables = []
    for parity in (0, 1):
        c, s = cos[parity::2, :half], sin[parity::2, :half]
        tables.append(np.block([[c, s], [-s, c]]).astype(ml_dtypes.bfloat16))
    return np.stack(tables)


def wavenumbers_squared(length):
    position = np.arange(length)
    signed = np.where(position < length // 2, position, position - length)
    wave = signed.astype(np.float32) * np.float32(2.0 * math.pi / length)
    squared = wave * wave
    return np.concatenate([squared[0::2], squared[1::2]])


Q_MAX = 14.0


def fit(function, degree):
    cheb = np.polynomial.chebyshev.Chebyshev.interpolate(
        lambda t: function((t + 1.0) * Q_MAX / 2), degree
    )
    return [float(v) for v in np.polynomial.chebyshev.cheb2poly(cheb.coef)]


COS_FIT = fit(lambda q: np.cos(np.sqrt(q)), 9)
SINC_FIT = fit(lambda q: np.sinc(np.sqrt(q) / np.pi), 9)


def horner(coefficients, t):
    total = jnp.full_like(t, coefficients[-1])
    for value in coefficients[-2::-1]:
        total = total * t + value
    return total


def cos_sin(square, root):
    t = square * (2.0 / Q_MAX) - 1.0
    return horner(COS_FIT, t), horner(SINC_FIT, t) * root


def lookup(table_row, codes):
    rows = codes.shape[0]
    parts = []
    for tile in range(codes.shape[1] // LANES):
        index = codes[:, tile * LANES : (tile + 1) * LANES]
        source = jnp.broadcast_to(table_row, (rows, LANES))
        parts.append(jnp.take_along_axis(source, index, axis=1, mode="promise_in_bounds"))
    return parts


def chain_kernel(
    place, angular_ref, source, receiver, code_own, code_core, code_y_same, code_y_cross,
    levels, left_x, right_x, left_y, right_y, wave_x, wave_y, *rest, strips, width, planes, shots,
):
    outs, (field, mid, padded) = rest[:-3], rest[-3:]
    tiles = len(outs) // 4
    own, same, core, cross = (outs[i * tiles : (i + 1) * tiles] for i in range(4))
    rows_x, rows_y = field.shape[1], field.shape[2]
    half_x, half_y = rows_x // 2, rows_y // 2
    first, my_core, my_parity = place[0], place[1], place[2]
    angular = angular_ref[0]
    f32, bf16 = jnp.float32, jnp.bfloat16

    field[0:2] = source[0, 0]
    field[2:4] = receiver[0, 0]
    padded[:, :, 0:HALO] = jnp.zeros((4, tiles, HALO, LANES), f32)
    padded[:, :, HALO + rows_x :] = jnp.zeros((4, tiles, HALO, LANES), f32)

    def step(t, carry):
        late = t >= planes - shots
        matched = lax.rem(t, shots) == my_core

        def codes_at(rows, cols):
            a = jnp.where(matched, code_own[rows, cols], code_core[rows, cols])
            b = jnp.where(matched, code_y_same[rows, cols], code_y_cross[rows, cols])
            return jnp.where(late, a, b).astype(f32).astype(jnp.int32)

        block = 64

        def add_block(i, total):
            rows = pl.ds(pl.multiple_of(i * block, block), block)
            parts = lookup(levels[0:1, :], codes_at(rows, slice(None)))
            value = functools.reduce(jnp.add, parts)
            return total + jnp.sum(value.reshape(block // 8, 8, LANES), axis=0)

        total = lax.fori_loop(0, rows_x // block, add_block, jnp.zeros((8, LANES), f32))
        base = jnp.sum(total) / (rows_x * rows_y)
        angle = angular * (levels[0:1, :] - base)
        screen_cos, screen_sin = cos_sin(angle * angle, angle)
        reach = angular * base
        reach = reach * reach

        def forward_x(i, carry):
            cols = pl.ds(pl.multiple_of(i * half_y, half_y), half_y)
            for kind in range(2):
                low = field[2 * kind : 2 * kind + 2, 0:half_x, cols].reshape(rows_x, half_y)
                high = field[2 * kind : 2 * kind + 2, half_x:, cols].reshape(rows_x, half_y)
                for parity, mixed in enumerate((low + high, low - high)):
                    out = jnp.dot(left_x[parity], mixed, preferred_element_type=f32).astype(bf16)
                    mid[2 * kind : 2 * kind + 2, parity * half_x : (parity + 1) * half_x, cols] = (
                        out.reshape(2, half_x, half_y)
                    )
            return carry

        lax.fori_loop(0, 2, forward_x, 0)

        rows_block = half_x // 2

        def along_y(i, carry):
            rows = pl.ds(pl.multiple_of(i * rows_block, rows_block), rows_block)
            blocks = mid[:, rows, :]
            low = jnp.concatenate(
                [jnp.concatenate([blocks[2 * k], blocks[2 * k + 1]], axis=1) for k in range(2)], axis=0
            )
            re = jnp.concatenate([blocks[0], blocks[2]], axis=0)
            im = jnp.concatenate([blocks[1], blocks[3]], axis=0)
            del low
            low = jnp.concatenate([re[:, :half_y], im[:, :half_y]], axis=1)
            high = jnp.concatenate([re[:, half_y:], im[:, half_y:]], axis=1)
            back = []
            for parity, mixed in enumerate((low + high, low - high)):
                spectrum = jnp.dot(mixed, right_y[parity], preferred_element_type=f32)
                q = reach - wave_x[rows, :] - wave_y[0:1, parity * half_y : (parity + 1) * half_y]
                root = jnp.sqrt(jnp.abs(q))
                cos, sin = cos_sin(q, root)
                phase_re = jnp.where(q > 0.0, cos, jnp.exp(-root))
                phase_im = jnp.where(q > 0.0, sin, 0.0)
                pieces = []
                for kind, sign in ((0, 1.0), (1, -1.0)):
                    part = spectrum[kind * rows_block : (kind + 1) * rows_block]
                    a, b = part[:, :half_y], part[:, half_y:]
                    if kind == 0:
                        pieces.append(
                            jnp.concatenate(
                                [a * phase_re - b * phase_im, a * phase_im + b * phase_re], axis=1
                            ).astype(bf16)
                        )
                    else:
                        pieces.append(
                            jnp.concatenate(
                                [a * phase_re + b * phase_im, b * phase_re - a * phase_im], axis=1
                            ).astype(bf16)
                        )
                shifted = jnp.concatenate(pieces, axis=0)
                back.append(jnp.dot(shifted, left_y[parity], preferred_element_type=f32))
            low = (back[0] + back[1]).astype(bf16)
            high = (back[0] - back[1]).astype(bf16)
            for kind in range(2):
                part = slice(kind * rows_block, (kind + 1) * rows_block)
                mid[2 * kind, rows, 0:half_y] = low[part, :half_y]
                mid[2 * kind, rows, half_y:] = high[part, :half_y]
                mid[2 * kind + 1, rows, 0:half_y] = low[part, half_y:]
                mid[2 * kind + 1, rows, half_y:] = high[part, half_y:]
            return carry

        lax.fori_loop(0, rows_x // rows_block, along_y, 0)

        def inverse_x(i, carry):
            cols = pl.ds(pl.multiple_of(i * LANES, LANES), LANES)
            turn = []
            for part in range(2):
                codes = codes_at(slice(part * half_x, (part + 1) * half_x), cols)
                turn.append((lookup(screen_cos, codes)[0], lookup(screen_sin, codes)[0]))
            for kind in range(2):
                even, odd = (
                    jnp.dot(
                        right_x[parity],
                        mid[
                            2 * kind : 2 * kind + 2, parity * half_x : (parity + 1) * half_x, cols
                        ].reshape(rows_x, LANES),
                        preferred_element_type=f32,
                    )
                    for parity in range(2)
                )
                for part, value in enumerate((even + odd, even - odd)):
                    a, b = value[:half_x], value[half_x:]
                    cos, sin = turn[part]
                    if kind == 0:
                        new_re, new_im = a * cos - b * sin, a * sin + b * cos
                    else:
                        new_re, new_im = a * cos + b * sin, b * cos - a * sin
                    rows = slice(part * half_x, (part + 1) * half_x)
                    field[2 * kind, rows, cols] = new_re.astype(bf16)
                    field[2 * kind + 1, rows, cols] = new_im.astype(bf16)
                    spot = slice(HALO + part * half_x, HALO + (part + 1) * half_x)
                    padded[2 * kind, i, spot] = new_re
                    padded[2 * kind + 1, i, spot] = new_im
            return carry

        lax.fori_loop(0, tiles, inverse_x, 0)

        def emit(targets, parity):
            def one(s, carry):
                start = pl.multiple_of((2 * s + parity) * width, 8)
                for tile in range(tiles):
                    for part in range(4):
                        targets[tile][part, s] = padded[
                            part, tile, pl.ds(start, width + 2 * HALO)
                        ].astype(bf16)
                return carry

            lax.fori_loop(0, strips, one, 0)

        @pl.when(late & matched)
        def _():
            emit(own, my_parity)
            emit(same, 1 - my_parity)

        @pl.when(late & jnp.logical_not(matched))
        def _():
            emit(core, my_parity)
            emit(cross, 1 - my_parity)

        return carry

    lax.fori_loop(first, planes, step, 0)


def correlate_kernel(order, *refs, width, partial, scale):
    del order
    fields, refs = refs[:4], refs[4:]
    received = None
    if partial:
        received, refs = refs[0], refs[1:]
    out, wide = refs[-2], refs[-1]
    for m in range(4):
        for part in range(4):
            wide[m * 4 + part] = fields[m][part, 0].astype(jnp.float32)
    for lag in range(2 * LAG + 1):
        shift = lag - LAG
        total = None
        for m in range(4):
            for part in range(2):
                term = (
                    wide[m * 4 + part, HALO - shift : HALO - shift + width]
                    * wide[m * 4 + 2 + part, HALO + shift : HALO + shift + width]
                )
                total = term if total is None else total + term
        if received is not None:
            total = total + received[lag].astype(jnp.float32)
        if scale is not None:
            out[0, lag] = total * scale
        else:
            out[lag] = total.astype(out.dtype)


def shards(source_top, receiver_top, slowness_codes, slowness_table, anchors):
    shots, _, _, rows_x, rows_y = source_top.shape
    freq_count = lax.axis_size("freq")
    depth_count = lax.axis_size("depth")
    planes = depth_count
    strips = freq_count // 2
    width = rows_x // freq_count
    lags = 2 * LAG + 1
    tiles = rows_y // LANES
    factor = 1.0 / math.sqrt(2.0 * shots * freq_count)
    depth_index = lax.axis_index("depth")
    freq_index = lax.axis_index("freq")
    my_core = depth_index % shots
    group = depth_index // shots
    my_parity = freq_index % 2
    bf16, f32 = jnp.bfloat16, jnp.float32

    def number(group_at, core_at, strip_at, parity_at):
        return (group_at * shots + core_at) * freq_count + strip_at * 2 + parity_at

    def pairs(move):
        found = []
        for g in range(depth_count // shots):
            for c in range(shots):
                for z in range(strips):
                    for x in range(2):
                        to = move(g, c, z, x)
                        if to is not None:
                            found.append((number(g, c, z, x), number(*to)))
        return found

    to_core = pairs(lambda g, c, z, x: (g, 1 - c, z, x))
    to_same = pairs(lambda g, c, z, x: (g, c, z, 1 - x))
    to_cross = pairs(lambda g, c, z, x: (g, 1 - c, z, 1 - x))
    up_same = pairs(lambda g, c, z, x: (1, c, z, x) if g == 0 else None)
    up_cross = pairs(lambda g, c, z, x: (1, 1 - c, z, x) if g == 0 else None)
    ring = [0] + list(range(1, strips, 2)) + list(range(2, strips, 2))[::-1]
    where = {z: p for p, z in enumerate(ring)}
    onward = pairs(lambda g, c, z, x: (g, c, ring[(where[z] + 1) % strips], x))
    plan = np.array(
        [[ring[(where[z] - 1 - s) % strips] for s in range(strips)] for z in range(strips)], np.int32
    )
    order = lax.dynamic_index_in_dim(jnp.asarray(plan), freq_index // 2, 0, keepdims=False)

    windows = [
        lax.dynamic_slice(
            slowness_codes[0], (anchors[s, 0], anchors[s, 1]), (rows_x, rows_y)
        ).astype(bf16)
        for s in range(shots)
    ]
    mine = jnp.where(my_core == 0, windows[0], windows[1])
    other = jnp.where(my_core == 0, windows[1], windows[0])
    code_y_same = lax.ppermute(mine, AXES, up_same)
    code_y_cross = lax.ppermute(other, AXES, up_cross)
    code_core = lax.ppermute(other, AXES, to_core)

    angular = math.pi * (0.45 + 0.5 * (freq_index.astype(f32) + 0.5) / freq_count)
    place = jnp.stack([(1 - group) * shots, my_core, my_parity]).astype(jnp.int32)
    levels = jnp.pad(slowness_table, (0, LANES - slowness_table.shape[0]))[None]
    tables_x, tables_y = parity_tables(rows_x), parity_tables(rows_y)
    wave_x = np.broadcast_to(wavenumbers_squared(rows_x)[:, None], (rows_x, 1))
    wave_y = wavenumbers_squared(rows_y)[None]
    height = width + 2 * HALO
    vmem = pl.BlockSpec(memory_space=pltpu.VMEM)
    top_spec = pl.BlockSpec(
        (1, 1, 2, rows_x, rows_y), lambda i, place, angular: (place[1], 0, 0, 0, 0)
    )
    outs = pl.pallas_call(
        functools.partial(
            chain_kernel, strips=strips, width=width, planes=planes, shots=shots
        ),
        out_shape=[jax.ShapeDtypeStruct((4, strips, height, LANES), bf16)] * (4 * tiles),
        grid_spec=pltpu.PrefetchScalarGridSpec(
            num_scalar_prefetch=2,
            grid=(1,),
            in_specs=[top_spec, top_spec] + [vmem] * 11,
            out_specs=[vmem] * (4 * tiles),
            scratch_shapes=[
                pltpu.VMEM((4, rows_x, rows_y), bf16),
                pltpu.VMEM((4, rows_x, rows_y), bf16),
                pltpu.VMEM((4, tiles, rows_x + 2 * HALO, LANES), f32),
            ],
        ),
        compiler_params=pltpu.CompilerParams(vmem_limit_bytes=VMEM_BYTES),
        name="chain",
    )(
        place,
        angular[None],
        source_top,
        receiver_top,
        mine,
        code_core,
        code_y_same,
        code_y_cross,
        levels,
        jnp.asarray(tables_x),
        jnp.asarray(np.swapaxes(tables_x, 1, 2)),
        jnp.asarray(tables_y),
        jnp.asarray(np.swapaxes(tables_y, 1, 2)),
        jnp.asarray(wave_x),
        jnp.asarray(wave_y),
    )

    def correlate(fields, received, step, buffer, tile):
        last = step == strips - 1
        field_spec = pl.BlockSpec((4, 1, height, LANES), lambda i, order: (0, order[step], 0, 0))
        in_specs = [field_spec] * 4
        operands = list(fields)
        image_spec = pl.BlockSpec((lags, width, LANES), lambda i, order: (0, 0, 0))
        if received is not None:
            in_specs.append(image_spec)
            operands.append(received)
        aliases = {}
        if last:
            out_shape = jax.ShapeDtypeStruct((1, lags, width, rows_y), f32)
            out_spec = pl.BlockSpec((1, lags, width, LANES), lambda i, order: (0, 0, 0, tile))
            if buffer is not None:
                in_specs.append(pl.BlockSpec(memory_space=pl.ANY))
                operands.append(buffer)
                aliases = {len(operands): 0}
        else:
            out_shape = jax.ShapeDtypeStruct((lags, width, LANES), bf16)
            out_spec = image_spec
        return pl.pallas_call(
            functools.partial(
                correlate_kernel,
                width=width,
                partial=received is not None,
                scale=factor if last else None,
            ),
            out_shape=out_shape,
            grid_spec=pltpu.PrefetchScalarGridSpec(
                num_scalar_prefetch=1,
                grid=(1,),
                in_specs=in_specs,
                out_specs=out_spec,
                scratch_shapes=[pltpu.VMEM((16, height, LANES), f32)],
            ),
            input_output_aliases=aliases,
            compiler_params=pltpu.CompilerParams(vmem_limit_bytes=16 * 2**20),
            cost_estimate=pl.CostEstimate(flops=10**8, bytes_accessed=2 * 10**6, transcendentals=0),
            name="correlate",
        )(order, *operands)

    image = None
    for tile in range(tiles):
        own, same, core, cross = (outs[i * tiles + tile] for i in range(4))
        fields = (
            own,
            lax.ppermute(same, AXES, to_same),
            lax.ppermute(core, AXES, to_core),
            lax.ppermute(cross, AXES, to_cross),
        )
        received = None
        for step in range(strips):
            result = correlate(fields, received, step, image, tile)
            if step < strips - 1:
                received = lax.ppermute(result, AXES, onward)
            else:
                image = result
    return image


def solution(mesh):
    return jax.shard_map(
        shards,
        mesh=mesh,
        in_specs=(
            P(None, "freq", None, None, None),
            P(None, "freq", None, None, None),
            P("depth", None, None),
            P(),
            P(),
        ),
        out_specs=P("depth", None, "freq", None),
        check_vma=False,
    )
```

```python
import functools
import math

import jax
import jax.numpy as jnp
import ml_dtypes
import numpy as np
from jax import lax
from jax.experimental import pallas as pl
from jax.experimental.pallas import tpu as pltpu
from jax.sharding import PartitionSpec as P

LAG = 7
HALO = 8
LANES = 128
AXES = ("depth", "freq")
VMEM_BYTES = 56 * 2**20


def parity_tables(length):
    position = np.arange(length, dtype=np.int64)
    product = position[:, None] * position[None, :] % length
    angles = product.astype(np.float32) * np.float32(2.0 * math.pi / length)
    factor = np.float32(1.0 / math.sqrt(length))
    cos, sin = np.cos(angles) * factor, np.sin(angles) * factor
    half = length // 2
    tables = []
    for parity in (0, 1):
        c, s = cos[parity::2, :half], sin[parity::2, :half]
        tables.append(np.block([[c, s], [-s, c]]).astype(ml_dtypes.bfloat16))
    return np.stack(tables)


def wavenumbers_squared(length):
    position = np.arange(length)
    signed = np.where(position < length // 2, position, position - length)
    wave = signed.astype(np.float32) * np.float32(2.0 * math.pi / length)
    squared = wave * wave
    return np.concatenate([squared[0::2], squared[1::2]])


Q_MAX = 14.0


def fit(function, degree):
    cheb = np.polynomial.chebyshev.Chebyshev.interpolate(
        lambda t: function((t + 1.0) * Q_MAX / 2), degree
    )
    return [float(v) for v in np.polynomial.chebyshev.cheb2poly(cheb.coef)]


COS_FIT = fit(lambda q: np.cos(np.sqrt(q)), 7)
SINC_FIT = fit(lambda q: np.sinc(np.sqrt(q) / np.pi), 7)


def horner(coefficients, t):
    total = jnp.full_like(t, coefficients[-1])
    for value in coefficients[-2::-1]:
        total = total * t + value
    return total


def cos_sin(square, root):
    t = square * (2.0 / Q_MAX) - 1.0
    return horner(COS_FIT, t), horner(SINC_FIT, t) * root


def lookup(table_row, codes):
    rows = codes.shape[0]
    parts = []
    for tile in range(codes.shape[1] // LANES):
        index = codes[:, tile * LANES : (tile + 1) * LANES]
        source = jnp.broadcast_to(table_row, (rows, LANES))
        parts.append(jnp.take_along_axis(source, index, axis=1, mode="promise_in_bounds"))
    return parts


def chain_kernel(
    place, order, angular_ref, *refs, begin, end, strips, width, tiles, shots, opening, closing,
):
    refs = list(refs)
    state = [refs.pop(0) for _ in range(2 if opening else 1)]
    codes = [refs.pop(0) for _ in range(end - begin)]
    levels, left_x, right_x, left_y, right_y, wave_x, wave_y = (refs.pop(0) for _ in range(7))
    padded = refs.pop() if closing else None
    mid = refs.pop()
    field = refs.pop() if closing else refs.pop(0)
    outs = refs
    rows_x, rows_y = field.shape[1], field.shape[2]
    half_x, half_y = rows_x // 2, rows_y // 2
    first, my_core, my_parity = place[0], place[1], place[2]
    angular = angular_ref[0]
    f32, bf16 = jnp.float32, jnp.bfloat16

    if opening:
        field[0:2] = state[0][0, 0]
        field[2:4] = state[1][0, 0]
    else:
        field[...] = state[0][...]
    if closing:
        padded[:, :, 0:HALO] = jnp.zeros((4, tiles, HALO, LANES), f32)
        padded[:, :, HALO + rows_x :] = jnp.zeros((4, tiles, HALO, LANES), f32)

    def step(t, carry):
        def codes_at(rows, cols):
            value = codes[end - begin - 1][rows, cols]
            for j in range(end - begin - 2, -1, -1):
                value = jnp.where(t == begin + j, codes[j][rows, cols], value)
            return value.astype(f32).astype(jnp.int32)

        def forward_x(i, carry):
            cols = pl.ds(pl.multiple_of(i * half_y, half_y), half_y)
            for part in range(2):
                index = codes_at(slice(part * half_x, (part + 1) * half_x), cols)
                value = functools.reduce(jnp.add, lookup(levels[0:1, :], index))
                carry = carry + jnp.sum(value.reshape(half_x // 8, 8, LANES), axis=0)
            for kind in range(2):
                low = field[2 * kind : 2 * kind + 2, 0:half_x, cols].reshape(rows_x, half_y)
                high = field[2 * kind : 2 * kind + 2, half_x:, cols].reshape(rows_x, half_y)
                for parity, mixed in enumerate((low + high, low - high)):
                    out = jnp.dot(left_x[parity], mixed, preferred_element_type=f32).astype(bf16)
                    mid[2 * kind : 2 * kind + 2, parity * half_x : (parity + 1) * half_x, cols] = (
                        out.reshape(2, half_x, half_y)
                    )
            return carry

        total = lax.fori_loop(0, 2, forward_x, jnp.zeros((8, LANES), f32))
        base = jnp.sum(total) / (rows_x * rows_y)
        angle = angular * (levels[0:1, :] - base)
        screen_cos, screen_sin = cos_sin(angle * angle, angle)
        reach = angular * base
        reach = reach * reach

        rows_block = half_x

        def along_y(i, carry):
            rows = pl.ds(pl.multiple_of(i * rows_block, rows_block), rows_block)
            blocks = mid[:, rows, :]
            re = jnp.concatenate([blocks[0], blocks[2]], axis=0)
            im = jnp.concatenate([blocks[1], blocks[3]], axis=0)
            low = jnp.concatenate([re[:, :half_y], im[:, :half_y]], axis=1)
            high = jnp.concatenate([re[:, half_y:], im[:, half_y:]], axis=1)
            back = []
            for parity, mixed in enumerate((low + high, low - high)):
                spectrum = jnp.dot(mixed, right_y[parity], preferred_element_type=f32)
                q = reach - wave_x[rows, :] - wave_y[0:1, parity * half_y : (parity + 1) * half_y]
                root = jnp.sqrt(jnp.abs(q))
                cos, sin = cos_sin(q, root)
                phase_re = jnp.where(q > 0.0, cos, jnp.exp(-root))
                phase_im = jnp.where(q > 0.0, sin, 0.0)
                pieces = []
                for kind, sign in ((0, 1.0), (1, -1.0)):
                    part = spectrum[kind * rows_block : (kind + 1) * rows_block]
                    a, b = part[:, :half_y], part[:, half_y:]
                    if kind == 0:
                        pieces.append(
                            jnp.concatenate(
                                [a * phase_re - b * phase_im, a * phase_im + b * phase_re], axis=1
                            ).astype(bf16)
                        )
                    else:
                        pieces.append(
                            jnp.concatenate(
                                [a * phase_re + b * phase_im, b * phase_re - a * phase_im], axis=1
                            ).astype(bf16)
                        )
                shifted = jnp.concatenate(pieces, axis=0)
                back.append(jnp.dot(shifted, left_y[parity], preferred_element_type=f32))
            low = (back[0] + back[1]).astype(bf16)
            high = (back[0] - back[1]).astype(bf16)
            for kind in range(2):
                part = slice(kind * rows_block, (kind + 1) * rows_block)
                mid[2 * kind, rows, 0:half_y] = low[part, :half_y]
                mid[2 * kind, rows, half_y:] = high[part, :half_y]
                mid[2 * kind + 1, rows, 0:half_y] = low[part, half_y:]
                mid[2 * kind + 1, rows, half_y:] = high[part, half_y:]
            return carry

        lax.fori_loop(0, rows_x // rows_block, along_y, 0)

        def inverse_x(i, carry):
            cols = pl.ds(pl.multiple_of(i * half_y, half_y), half_y)
            turn = []
            for part in range(2):
                codes = codes_at(slice(part * half_x, (part + 1) * half_x), cols)
                turn.append(tuple(jnp.concatenate(lookup(v, codes), axis=1) for v in (screen_cos, screen_sin)))
            for kind in range(2):
                even, odd = (
                    jnp.dot(
                        right_x[parity],
                        mid[
                            2 * kind : 2 * kind + 2, parity * half_x : (parity + 1) * half_x, cols
                        ].reshape(rows_x, half_y),
                        preferred_element_type=f32,
                    )
                    for parity in range(2)
                )
                for part, value in enumerate((even + odd, even - odd)):
                    a, b = value[:half_x], value[half_x:]
                    cos, sin = turn[part]
                    if kind == 0:
                        new_re, new_im = a * cos - b * sin, a * sin + b * cos
                    else:
                        new_re, new_im = a * cos + b * sin, b * cos - a * sin
                    rows = slice(part * half_x, (part + 1) * half_x)
                    field[2 * kind, rows, cols] = new_re.astype(bf16)
                    field[2 * kind + 1, rows, cols] = new_im.astype(bf16)
                    spot = slice(HALO + part * half_x, HALO + (part + 1) * half_x)
                    for j in range(half_y // LANES if closing else 0):
                        lanes = slice(j * LANES, (j + 1) * LANES)
                        padded[2 * kind, i * (half_y // LANES) + j, spot] = new_re[:, lanes]
                        padded[2 * kind + 1, i * (half_y // LANES) + j, spot] = new_im[:, lanes]
            return carry

        lax.fori_loop(0, 2, inverse_x, 0)

        if not closing:
            return carry

        def emit(target, parity):
            for s in range(strips):
                start = pl.multiple_of((2 * order[s] + parity) * width, 8)
                for tile in range(tiles):
                    half, at = divmod(tile, tiles // 2)
                    for part in range(4):
                        piece = padded[part, tile, pl.ds(start, width + 2 * HALO)]
                        outs[(target * strips + s) * 2 + half][part, at] = piece.astype(bf16)

        matched = t == end - shots + my_core

        @pl.when(matched)
        def _():
            emit(0, my_parity)
            emit(1, 1 - my_parity)

        @pl.when(jnp.logical_not(matched) & (t >= end - shots))
        def _():
            emit(2, my_parity)
            emit(3, 1 - my_parity)

        return carry

    lax.fori_loop(jnp.maximum(first, begin), end, step, 0)


def correlate_kernel(*refs, width, tiles, partial, scale):
    fields, refs = refs[:4], refs[4:]
    received = None
    if partial:
        received, refs = refs[0], refs[1:]
    out, wide = refs[-2], refs[-1]
    for tile in range(tiles):
        lanes = slice(tile * LANES, (tile + 1) * LANES)
        for m in range(4):
            for part in range(4):
                wide[m * 4 + part] = fields[m][part, tile].astype(jnp.float32)
        for lag in range(2 * LAG + 1):
            shift = lag - LAG
            total = None
            for m in range(4):
                for part in range(2):
                    term = (
                        wide[m * 4 + part, HALO - shift : HALO - shift + width]
                        * wide[m * 4 + 2 + part, HALO + shift : HALO + shift + width]
                    )
                    total = term if total is None else total + term
            if received is not None:
                total = total + received[lag, tile].astype(jnp.float32)
            if scale is not None:
                out[0, lag, :, lanes] = total * scale
            else:
                out[lag, tile] = total.astype(out.dtype)


def window_kernel(place, anchors, codes, out):
    del place, anchors
    out[...] = codes[0].astype(jnp.float32).astype(out.dtype)


def chain(
    place, order, angular, state, codes, table, begin, end, strips, width, shots, opening, closing
):
    rows_x, rows_y = state[0].shape[-2:]
    tiles = rows_y // LANES
    bf16, f32 = jnp.bfloat16, jnp.float32
    levels = jnp.pad(table, (0, LANES - table.shape[0]))[None]
    tables_x, tables_y = parity_tables(rows_x), parity_tables(rows_y)
    wave_x = np.broadcast_to(wavenumbers_squared(rows_x)[:, None], (rows_x, 1))
    wave_y = wavenumbers_squared(rows_y)[None]
    height = width + 2 * HALO
    vmem = pl.BlockSpec(memory_space=pltpu.VMEM)
    top_spec = pl.BlockSpec(
        (1, 1, 2, rows_x, rows_y), lambda i, place, order, angular: (place[1], 0, 0, 0, 0)
    )
    whole = (4, rows_x, rows_y)
    scratch = [pltpu.VMEM(whole, bf16)]
    if closing:
        out_shape = [jax.ShapeDtypeStruct((4, tiles // 2, height, LANES), bf16)] * (8 * strips)
        scratch = scratch + [
            pltpu.VMEM(whole, bf16),
            pltpu.VMEM((4, tiles, rows_x + 2 * HALO, LANES), f32),
        ]
    else:
        out_shape = [jax.ShapeDtypeStruct(whole, bf16)]
    return pl.pallas_call(
        functools.partial(
            chain_kernel, begin=begin, end=end, strips=strips, width=width, tiles=tiles,
            shots=shots, opening=opening, closing=closing,
        ),
        out_shape=out_shape,
        grid_spec=pltpu.PrefetchScalarGridSpec(
            num_scalar_prefetch=3,
            grid=(1,),
            in_specs=([top_spec] * 2 if opening else [vmem]) + [vmem] * (7 + len(codes)),
            out_specs=[vmem] * len(out_shape),
            scratch_shapes=scratch,
        ),
        compiler_params=pltpu.CompilerParams(vmem_limit_bytes=VMEM_BYTES),
        name="chain",
    )(
        place, order, angular, *state, *codes, levels,
        jnp.asarray(tables_x),
        jnp.asarray(np.swapaxes(tables_x, 1, 2)),
        jnp.asarray(tables_y),
        jnp.asarray(np.swapaxes(tables_y, 1, 2)),
        jnp.asarray(wave_x),
        jnp.asarray(wave_y),
    )


def shards(source_top, receiver_top, slowness_codes, slowness_table, anchors):
    shots, _, _, rows_x, rows_y = source_top.shape
    freq_count = lax.axis_size("freq")
    depth_count = lax.axis_size("depth")
    strips = freq_count // 2
    width = rows_x // freq_count
    lags = 2 * LAG + 1
    tiles = rows_y // LANES
    factor = 1.0 / math.sqrt(2.0 * shots * freq_count)
    depth_index = lax.axis_index("depth")
    freq_index = lax.axis_index("freq")
    my_core = depth_index % shots
    group = depth_index // shots
    my_parity = freq_index % 2
    bf16, f32 = jnp.bfloat16, jnp.float32

    def number(group_at, core_at, strip_at, parity_at):
        return (group_at * shots + core_at) * freq_count + strip_at * 2 + parity_at

    def pairs(move):
        found = []
        for g in range(depth_count // shots):
            for c in range(shots):
                for z in range(strips):
                    for x in range(2):
                        to = move(g, c, z, x)
                        if to is not None:
                            found.append((number(g, c, z, x), number(*to)))
        return found

    to_core = pairs(lambda g, c, z, x: (g, 1 - c, z, x))
    to_same = pairs(lambda g, c, z, x: (g, c, z, 1 - x))
    to_cross = pairs(lambda g, c, z, x: (g, 1 - c, z, 1 - x))
    up = pairs(lambda g, c, z, x: (1, c, z, x) if g == 0 else None)
    ring = [0] + list(range(1, strips, 2)) + list(range(2, strips, 2))[::-1]
    where = {z: p for p, z in enumerate(ring)}
    onward = pairs(lambda g, c, z, x: (g, c, ring[(where[z] + 1) % strips], x))
    plan = np.array(
        [[ring[(where[z] - 1 - s) % strips] for s in range(strips)] for z in range(strips)], np.int32
    )
    order = lax.dynamic_index_in_dim(jnp.asarray(plan), freq_index // 2, 0, keepdims=False)
    place = jnp.stack([(1 - group) * shots, my_core, my_parity]).astype(jnp.int32)

    def window(flip):
        def block(i, place, anchors):
            shot = jnp.abs(place[1] - flip)
            return (0, anchors[shot, 0] // rows_x, anchors[shot, 1] // rows_y)

        return pl.pallas_call(
            window_kernel,
            out_shape=jax.ShapeDtypeStruct((rows_x, rows_y), bf16),
            grid_spec=pltpu.PrefetchScalarGridSpec(
                num_scalar_prefetch=2,
                grid=(1,),
                in_specs=[pl.BlockSpec((1, rows_x, rows_y), block)],
                out_specs=pl.BlockSpec((rows_x, rows_y), lambda i, place, anchors: (0, 0)),
            ),
            name="window",
        )(place, anchors, slowness_codes)

    other = window(1)
    mine = window(0)
    from_core = lax.ppermute(other, AXES, to_core)
    near = [jnp.where(my_core == p, mine, from_core) for p in range(shots)]
    far = [lax.ppermute(near[p], AXES, up) for p in range(shots)]

    angular = math.pi * (0.45 + 0.5 * (freq_index.astype(f32) + 0.5) / freq_count)
    common = dict(strips=strips, width=width, shots=shots)
    start = (place, order, angular[None])
    state = chain(
        *start, (source_top, receiver_top), far[:1], slowness_table, 0, 1,
        opening=True, closing=False, **common,
    )
    outs = chain(
        *start, state, far[1:] + near, slowness_table, 1, 2 * shots,
        opening=False, closing=True, **common,
    )
    height = width + 2 * HALO

    def correlate(fields, received, last, buffer, half):
        operands = list(fields)
        field_spec = pl.BlockSpec((4, tiles // 2, height, LANES), lambda i: (0, 0, 0, 0))
        image_spec = pl.BlockSpec((lags, tiles // 2, width, LANES), lambda i: (0, 0, 0, 0))
        in_specs = [field_spec] * 4
        if received is not None:
            in_specs.append(image_spec)
            operands.append(received)
        aliases = {}
        if last:
            out_shape = jax.ShapeDtypeStruct((1, lags, width, rows_y), f32)
            out_spec = pl.BlockSpec((1, lags, width, rows_y // 2), lambda i: (0, 0, 0, half))
            if buffer is not None:
                in_specs.append(pl.BlockSpec(memory_space=pl.ANY))
                aliases = {len(operands): 0}
                operands.append(buffer)
        else:
            out_shape = jax.ShapeDtypeStruct((lags, tiles // 2, width, LANES), bf16)
            out_spec = image_spec
        return pl.pallas_call(
            functools.partial(
                correlate_kernel,
                width=width,
                tiles=tiles // 2,
                partial=received is not None,
                scale=factor if last else None,
            ),
            out_shape=out_shape,
            grid=(1,),
            in_specs=in_specs,
            out_specs=out_spec,
            scratch_shapes=[pltpu.VMEM((16, height, LANES), f32)],
            input_output_aliases=aliases,
            compiler_params=pltpu.CompilerParams(vmem_limit_bytes=16 * 2**20),
            cost_estimate=pl.CostEstimate(flops=10**9, bytes_accessed=6 * 10**6, transcendentals=0),
            name="correlate",
        )(*operands)

    def fetch(step, half):
        own, same, core, cross = (outs[(i * strips + step) * 2 + half] for i in range(4))
        return (
            own,
            lax.ppermute(same, AXES, to_same),
            lax.ppermute(core, AXES, to_core),
            lax.ppermute(cross, AXES, to_cross),
        )

    image = None
    received = [None, None]
    for step in range(strips):
        for half in range(2):
            last = step == strips - 1
            result = correlate(fetch(step, half), received[half], last, image, half)
            if last:
                image = result
            else:
                received[half] = lax.ppermute(result, AXES, onward)
    return image


def solution(mesh):
    return jax.shard_map(
        shards,
        mesh=mesh,
        in_specs=(
            P(None, "freq", None, None, None),
            P(None, "freq", None, None, None),
            P("depth", None, None),
            P(),
            P(),
        ),
        out_specs=P("depth", None, "freq", None),
        check_vma=False,
    )
```

```python
import functools
import math

import jax
import jax.numpy as jnp
import ml_dtypes
import numpy as np
from jax import lax
from jax.experimental import pallas as pl
from jax.experimental.pallas import tpu as pltpu
from jax.sharding import PartitionSpec as P

LAG = 7
HALO = 8
LANES = 128
AXES = ("depth", "freq")
VMEM_BYTES = 56 * 2**20


def parity_tables(length):
    position = np.arange(length, dtype=np.int64)
    product = position[:, None] * position[None, :] % length
    angles = product.astype(np.float32) * np.float32(2.0 * math.pi / length)
    factor = np.float32(1.0 / math.sqrt(length))
    cos, sin = np.cos(angles) * factor, np.sin(angles) * factor
    half = length // 2
    tables = []
    for parity in (0, 1):
        c, s = cos[parity::2, :half], sin[parity::2, :half]
        tables.append(np.block([[c, s], [-s, c]]).astype(ml_dtypes.bfloat16))
    return np.stack(tables)


def wavenumbers_squared(length):
    position = np.arange(length)
    signed = np.where(position < length // 2, position, position - length)
    wave = signed.astype(np.float32) * np.float32(2.0 * math.pi / length)
    squared = wave * wave
    return np.concatenate([squared[0::2], squared[1::2]])


Q_MAX = 14.0


def fit(function, degree):
    cheb = np.polynomial.chebyshev.Chebyshev.interpolate(
        lambda t: function((t + 1.0) * Q_MAX / 2), degree
    )
    return [float(v) for v in np.polynomial.chebyshev.cheb2poly(cheb.coef)]


COS_FIT = fit(lambda q: np.cos(np.sqrt(q)), 7)
SINC_FIT = fit(lambda q: np.sinc(np.sqrt(q) / np.pi), 7)


def horner(coefficients, t):
    total = jnp.full_like(t, coefficients[-1])
    for value in coefficients[-2::-1]:
        total = total * t + value
    return total


def cos_sin(square, root):
    t = square * (2.0 / Q_MAX) - 1.0
    return horner(COS_FIT, t), horner(SINC_FIT, t) * root


def lookup(table_row, codes):
    rows = codes.shape[0]
    parts = []
    for tile in range(codes.shape[1] // LANES):
        index = codes[:, tile * LANES : (tile + 1) * LANES]
        source = jnp.broadcast_to(table_row, (rows, LANES))
        parts.append(jnp.take_along_axis(source, index, axis=1, mode="promise_in_bounds"))
    return parts


def pick(flag, pair, *where):
    return jnp.where(flag, pair[0][where], pair[1][where])


def codes_of(flag, pair, rows, cols):
    return pick(flag, pair, rows, cols).astype(jnp.float32).astype(jnp.int32)


def chain_kernel(
    place, angular_ref, *refs, top, screened, planes, closing, strips, width, tiles, groups, shots
):
    refs = list(refs)

    def take(count):
        return [refs.pop(0) for _ in range(count)]

    tops = take(2) if top else None
    if screened:
        (before,) = take(1)
        before_codes, before_means = take(2), take(2)
    codes = [take(2) for _ in range(planes)] if closing else None
    means = [take(2) for _ in range(planes)]
    levels, left_x, right_x, left_y, right_y, wave_x, wave_y = take(7)
    if closing:
        field, mid, padded = refs[-3:]
        outs = refs[:-3]
    else:
        after, field, mid = refs
    rows_x, rows_y = field.shape[1], field.shape[2]
    half_x, half_y = rows_x // 2, rows_y // 2
    group, my_core, my_parity, spot = place[0], place[1], place[2], place[3]
    angular = angular_ref[0]
    f32, bf16 = jnp.float32, jnp.bfloat16
    lower_planes = group == 0

    def screen_table(mean):
        angle = angular * (levels[0:1, :] - mean)
        return cos_sin(angle * angle, angle)

    def turned(kind, a, b, cos, sin):
        if kind == 0:
            return a * cos - b * sin, a * sin + b * cos
        return a * cos + b * sin, b * cos - a * sin

    def load_top():
        field[0:2] = tops[0][0, 0]
        field[2:4] = tops[1][0, 0]

    def load_screened(index):
        flag = index == my_core
        tables = screen_table(pick(flag, before_means))

        def block(i, carry):
            rows = pl.ds(pl.multiple_of(i * 64, 64), 64)
            at = codes_of(flag, before_codes, rows, slice(None))
            cos, sin = (jnp.concatenate(lookup(table, at), axis=1) for table in tables)
            for kind in range(2):
                re, im = turned(kind, before[2 * kind, rows], before[2 * kind + 1, rows], cos, sin)
                field[2 * kind, rows] = re.astype(bf16)
                field[2 * kind + 1, rows] = im.astype(bf16)
            return carry

        lax.fori_loop(0, rows_x // 64, block, 0)

    def transforms(mean, sink):
        reach = angular * mean[0:1, 0:1]
        reach = reach * reach

        def forward_x(i, carry):
            cols = pl.ds(pl.multiple_of(i * half_y, half_y), half_y)
            for kind in range(2):
                low = field[2 * kind : 2 * kind + 2, 0:half_x, cols].reshape(rows_x, half_y)
                high = field[2 * kind : 2 * kind + 2, half_x:, cols].reshape(rows_x, half_y)
                for parity, mixed in enumerate((low + high, low - high)):
                    out = jnp.dot(left_x[parity], mixed, preferred_element_type=f32).astype(bf16)
                    mid[2 * kind : 2 * kind + 2, parity * half_x : (parity + 1) * half_x, cols] = (
                        out.reshape(2, half_x, half_y)
                    )
            return carry

        lax.fori_loop(0, 2, forward_x, 0)

        def along_y(i, carry):
            rows = pl.ds(pl.multiple_of(i * half_x, half_x), half_x)
            blocks = mid[:, rows, :]
            re = jnp.concatenate([blocks[0], blocks[2]], axis=0)
            im = jnp.concatenate([blocks[1], blocks[3]], axis=0)
            low = jnp.concatenate([re[:, :half_y], im[:, :half_y]], axis=1)
            high = jnp.concatenate([re[:, half_y:], im[:, half_y:]], axis=1)
            back = []
            for parity, mixed in enumerate((low + high, low - high)):
                spectrum = jnp.dot(mixed, right_y[parity], preferred_element_type=f32)
                q = reach - wave_x[rows, :] - wave_y[0:1, parity * half_y : (parity + 1) * half_y]
                root = jnp.sqrt(jnp.abs(q))
                cos, sin = cos_sin(q, root)
                phase_re = jnp.where(q > 0.0, cos, jnp.exp(-root))
                phase_im = jnp.where(q > 0.0, sin, 0.0)
                pieces = []
                for kind in range(2):
                    part = spectrum[kind * half_x : (kind + 1) * half_x]
                    new = turned(kind, part[:, :half_y], part[:, half_y:], phase_re, phase_im)
                    pieces.append(jnp.concatenate(new, axis=1).astype(bf16))
                shifted = jnp.concatenate(pieces, axis=0)
                back.append(jnp.dot(shifted, left_y[parity], preferred_element_type=f32))
            low = (back[0] + back[1]).astype(bf16)
            high = (back[0] - back[1]).astype(bf16)
            for kind in range(2):
                part = slice(kind * half_x, (kind + 1) * half_x)
                mid[2 * kind, rows, 0:half_y] = low[part, :half_y]
                mid[2 * kind, rows, half_y:] = high[part, :half_y]
                mid[2 * kind + 1, rows, 0:half_y] = low[part, half_y:]
                mid[2 * kind + 1, rows, half_y:] = high[part, half_y:]
            return carry

        lax.fori_loop(0, 2, along_y, 0)

        def inverse_x(i, carry):
            cols = pl.ds(pl.multiple_of(i * half_y, half_y), half_y)
            give = sink(i, cols)
            for kind in range(2):
                even, odd = (
                    jnp.dot(
                        right_x[parity],
                        mid[
                            2 * kind : 2 * kind + 2, parity * half_x : (parity + 1) * half_x, cols
                        ].reshape(rows_x, half_y),
                        preferred_element_type=f32,
                    )
                    for parity in range(2)
                )
                for part, value in enumerate((even + odd, even - odd)):
                    give(kind, part, value[:half_x], value[half_x:])
            return carry

        lax.fori_loop(0, 2, inverse_x, 0)

    def rows_of(part):
        return slice(part * half_x, (part + 1) * half_x)

    def sink_plain(i, cols):
        def give(kind, part, a, b):
            after[2 * kind, rows_of(part), cols] = a
            after[2 * kind + 1, rows_of(part), cols] = b

        return give

    def sink_screened(tables, flag, pair):
        def sink(i, cols):
            turn = []
            for part in range(2):
                at = codes_of(flag, pair, rows_of(part), cols)
                turn.append([jnp.concatenate(lookup(table, at), axis=1) for table in tables])

            def give(kind, part, a, b):
                for j, value in enumerate(turned(kind, a, b, *turn[part])):
                    field[2 * kind + j, rows_of(part), cols] = value.astype(bf16)
                    start = HALO + part * half_x
                    for k in range(half_y // LANES):
                        padded[2 * kind + j, i * (half_y // LANES) + k, start : start + half_x] = (
                            value[:, k * LANES : (k + 1) * LANES]
                        )

            return give

        return sink

    def emit(target, parity):
        for s in range(strips):
            p = lax.rem(spot + (strips - 1 - s), strips)
            strip = jnp.where(p == 0, 0, jnp.where(p <= strips // 2, 2 * p - 1, 2 * (strips - p)))
            start = pl.multiple_of((2 * strip + parity) * width, 8)
            for g, (first, last) in enumerate(groups):
                for tile in range(first, last):
                    for part in range(4):
                        piece = padded[part, tile, pl.ds(start, width + 2 * HALO)]
                        outs[(target * strips + s) * len(groups) + g][part, tile - first] = (
                            piece.astype(bf16)
                        )

    if not closing:

        @pl.when(jnp.logical_not(lower_planes))
        def _():
            index = 0
            if screened:
                load_screened(0)
                index = 1
            else:
                load_top()
            transforms(pick(index == my_core, means[0]), sink_plain)

        return

    @pl.when(lower_planes)
    def _():
        load_top()

    @pl.when(jnp.logical_not(lower_planes))
    def _():
        load_screened(shots - 1)

    padded[:, :, 0:HALO] = jnp.zeros((4, tiles, HALO, LANES), f32)
    padded[:, :, HALO + rows_x :] = jnp.zeros((4, tiles, HALO, LANES), f32)
    for t in range(planes):
        flag = my_core == t
        mean = pick(flag, means[t])
        transforms(mean, sink_screened(screen_table(mean), flag, codes[t]))

        @pl.when(flag)
        def _():
            emit(0, my_parity)
            emit(1, 1 - my_parity)

        @pl.when(jnp.logical_not(flag))
        def _():
            emit(2, my_parity)
            emit(3, 1 - my_parity)


def correlate_kernel(*refs, width, tiles, partial, scale):
    fields, refs = refs[:4], refs[4:]
    received = None
    if partial:
        received, refs = refs[0], refs[1:]
    out, wide = refs[-2], refs[-1]
    for tile in range(tiles):
        lanes = slice(tile * LANES, (tile + 1) * LANES)
        for m in range(4):
            for part in range(4):
                wide[m * 4 + part] = fields[m][part, tile].astype(jnp.float32)
        for lag in range(2 * LAG + 1):
            shift = lag - LAG
            total = None
            for m in range(4):
                for part in range(2):
                    term = (
                        wide[m * 4 + part, HALO - shift : HALO - shift + width]
                        * wide[m * 4 + 2 + part, HALO + shift : HALO + shift + width]
                    )
                    total = term if total is None else total + term
            if received is not None:
                total = total + received[lag, tile].astype(jnp.float32)
            if scale is not None:
                out[0, lag, :, lanes] = total * scale
            else:
                out[lag, tile] = total.astype(out.dtype)


def window_kernel(place, anchors, mine, other, table, *refs, cells):
    del place, anchors
    out_mine, out_other, mean_mine, mean_other, levels = refs
    levels[0:1, 0 : table.shape[1]] = table[...]
    i = pl.program_id(0)
    for codes, out, mean in ((mine, out_mine, mean_mine), (other, out_other, mean_other)):
        out[...] = codes[0].astype(jnp.float32).astype(out.dtype)
        value = functools.reduce(jnp.add, lookup(levels[0:1, :], codes[0]))
        value = jnp.sum(value, axis=0, keepdims=True)

        @pl.when(i == 0)
        def _(value=value, mean=mean):
            mean[...] = value

        @pl.when(i > 0)
        def _(value=value, mean=mean):
            mean[...] += value

        @pl.when(i == pl.num_programs(0) - 1)
        def _(mean=mean):
            mean[...] = jnp.broadcast_to(
                jnp.sum(mean[...], axis=1, keepdims=True) / cells, mean.shape
            )


def chain(
    place, angular, table, *, tops=None, before=None, codes=(), means=(), strips, width, groups, shots
):
    closing = bool(codes)
    rows_x, rows_y = (tops[0] if tops else before[0]).shape[-2:]
    tiles = rows_y // LANES
    bf16, f32 = jnp.bfloat16, jnp.float32
    tables_x, tables_y = parity_tables(rows_x), parity_tables(rows_y)
    wave_x = np.broadcast_to(wavenumbers_squared(rows_x)[:, None], (rows_x, 1))
    wave_y = wavenumbers_squared(rows_y)[None]
    height = width + 2 * HALO
    vmem = pl.BlockSpec(memory_space=pltpu.VMEM)
    top_spec = pl.BlockSpec(
        (1, 1, 2, rows_x, rows_y), lambda i, place, angular: (place[1], 0, 0, 0, 0)
    )
    operands = []
    in_specs = []
    if tops:
        operands += list(tops)
        in_specs += [top_spec] * 2
    if before:
        state, before_codes, before_means = before
        operands += [state, *before_codes, *before_means]
    for pair in (*codes, *means):
        operands += list(pair)
    operands += [
        jnp.pad(table, (0, LANES - table.shape[0]))[None],
        jnp.asarray(tables_x),
        jnp.asarray(np.swapaxes(tables_x, 1, 2)),
        jnp.asarray(tables_y),
        jnp.asarray(np.swapaxes(tables_y, 1, 2)),
        jnp.asarray(wave_x),
        jnp.asarray(wave_y),
    ]
    in_specs += [vmem] * (len(operands) - len(in_specs))
    whole = (4, rows_x, rows_y)
    scratch = [pltpu.VMEM(whole, bf16), pltpu.VMEM(whole, bf16)]
    if closing:
        out_shape = [
            jax.ShapeDtypeStruct((4, last - first, height, LANES), bf16)
            for _ in range(4 * strips)
            for first, last in groups
        ]
        scratch.append(pltpu.VMEM((4, tiles, rows_x + 2 * HALO, LANES), f32))
    else:
        out_shape = [jax.ShapeDtypeStruct(whole, f32)]
    return pl.pallas_call(
        functools.partial(
            chain_kernel, top=bool(tops), screened=bool(before), planes=len(means), closing=closing,
            strips=strips, width=width, tiles=tiles, groups=groups, shots=shots,
        ),
        out_shape=out_shape,
        grid_spec=pltpu.PrefetchScalarGridSpec(
            num_scalar_prefetch=2,
            grid=(1,),
            in_specs=in_specs,
            out_specs=[vmem] * len(out_shape),
            scratch_shapes=scratch,
        ),
        compiler_params=pltpu.CompilerParams(vmem_limit_bytes=VMEM_BYTES),
        cost_estimate=pl.CostEstimate(
            flops=9 * 10**9 * len(means), bytes_accessed=10**7, transcendentals=0
        ),
        name="chain",
    )(place, angular, *operands)


def windows(place, anchors, slowness_codes, table, rows_x, rows_y):
    steps = 8
    rows = rows_x // steps

    def block(flip):
        def index(i, place, anchors):
            shot = jnp.abs(place[1] - flip)
            return (0, anchors[shot, 0] // rows + i, anchors[shot, 1] // rows_y)

        return pl.BlockSpec((1, rows, rows_y), index)

    code_shape = jax.ShapeDtypeStruct((rows_x, rows_y), jnp.bfloat16)
    mean_shape = jax.ShapeDtypeStruct((1, LANES), jnp.float32)
    code_spec = pl.BlockSpec((rows, rows_y), lambda i, place, anchors: (i, 0))
    mean_spec = pl.BlockSpec((1, LANES), lambda i, place, anchors: (0, 0))
    return pl.pallas_call(
        functools.partial(window_kernel, cells=rows_x * rows_y),
        out_shape=[code_shape, code_shape, mean_shape, mean_shape],
        grid_spec=pltpu.PrefetchScalarGridSpec(
            num_scalar_prefetch=2,
            grid=(steps,),
            in_specs=[
                block(0),
                block(1),
                pl.BlockSpec((1, table.shape[0]), lambda i, place, anchors: (0, 0)),
            ],
            out_specs=[code_spec, code_spec, mean_spec, mean_spec],
            scratch_shapes=[pltpu.VMEM((8, LANES), jnp.float32)],
        ),
        name="windows",
    )(place, anchors, slowness_codes, slowness_codes, table[None])


def shards(source_top, receiver_top, slowness_codes, slowness_table, anchors):
    shots, _, _, rows_x, rows_y = source_top.shape
    freq_count = lax.axis_size("freq")
    depth_count = lax.axis_size("depth")
    strips = freq_count // 2
    width = rows_x // freq_count
    lags = 2 * LAG + 1
    tiles = rows_y // LANES
    groups = [(0, tiles // 2), (tiles // 2, tiles)]
    factor = 1.0 / math.sqrt(2.0 * shots * freq_count)
    depth_index = lax.axis_index("depth")
    freq_index = lax.axis_index("freq")
    my_core = depth_index % shots
    group = depth_index // shots
    bf16, f32 = jnp.bfloat16, jnp.float32

    def number(group_at, core_at, strip_at, parity_at):
        return (group_at * shots + core_at) * freq_count + strip_at * 2 + parity_at

    def pairs(move):
        found = []
        for g in range(depth_count // shots):
            for c in range(shots):
                for z in range(strips):
                    for x in range(2):
                        to = move(g, c, z, x)
                        if to is not None:
                            found.append((number(g, c, z, x), number(*to)))
        return found

    def send(value, move):
        return lax.ppermute(value, AXES, pairs(move))

    def to_core(g, c, z, x):
        return (g, 1 - c, z, x)

    def to_same(g, c, z, x):
        return (g, c, z, 1 - x)

    def to_cross(g, c, z, x):
        return (g, 1 - c, z, 1 - x)

    def up(core):
        return lambda g, c, z, x: (1, c, z, x) if g == 0 and c == core else None

    def up_same(g, c, z, x):
        return (1, c, z, x) if g == 0 else None

    def up_cross(g, c, z, x):
        return (1, 1 - c, z, x) if g == 0 else None

    ring = [0] + list(range(1, strips, 2)) + list(range(2, strips, 2))[::-1]
    spots = {z: p for p, z in enumerate(ring)}

    def onward(g, c, z, x):
        return (g, c, ring[(spots[z] + 1) % strips], x)

    my_strip = freq_index // 2
    spot = jnp.where(
        my_strip == 0,
        0,
        jnp.where(my_strip % 2 == 1, (my_strip + 1) // 2, strips - my_strip // 2),
    )
    place = jnp.stack([group, my_core, freq_index % 2, spot]).astype(jnp.int32)

    mine, other, mean_mine, mean_other = windows(
        place, anchors, slowness_codes, slowness_table, rows_x, rows_y
    )
    far_means = (send(mean_mine, up_same), send(mean_other, up_cross))
    from_core = send(other, to_core)
    near_means = (mean_mine, send(mean_other, to_core))
    far_first = (send(mine, up(0)), send(from_core, up(1)))
    mine_later, from_core_later, _ = lax.optimization_barrier((mine, from_core, mean_mine))
    far_second = (send(mine_later, up(1)), send(from_core_later, up(0)))
    near = (mine, from_core)

    angular = (math.pi * (0.45 + 0.5 * (freq_index.astype(f32) + 0.5) / freq_count))[None]
    common = dict(strips=strips, width=width, groups=groups, shots=shots)
    tops = (source_top, receiver_top)
    (state,) = chain(place, angular, slowness_table, tops=tops, means=[far_means], **common)
    (state,) = chain(
        place, angular, slowness_table, before=(state, far_first, far_means), means=[far_means],
        **common,
    )
    outs = chain(
        place, angular, slowness_table, tops=tops, before=(state, far_second, far_means),
        codes=[near] * shots, means=[near_means] * shots, **common,
    )
    height = width + 2 * HALO

    def correlate(fields, received, last, buffer, g):
        first, end = groups[g]
        count = end - first
        operands = list(fields)
        field_spec = pl.BlockSpec((4, count, height, LANES), lambda i: (0, 0, 0, 0))
        image_spec = pl.BlockSpec((lags, count, width, LANES), lambda i: (0, 0, 0, 0))
        in_specs = [field_spec] * 4
        if received is not None:
            in_specs.append(image_spec)
            operands.append(received)
        aliases = {}
        if last:
            out_shape = jax.ShapeDtypeStruct((1, lags, width, rows_y), f32)
            out_spec = pl.BlockSpec(
                (1, lags, width, count * LANES), lambda i: (0, 0, 0, first // count)
            )
            if buffer is not None:
                in_specs.append(pl.BlockSpec(memory_space=pl.ANY))
                aliases = {len(operands): 0}
                operands.append(buffer)
        else:
            out_shape = jax.ShapeDtypeStruct((lags, count, width, LANES), bf16)
            out_spec = image_spec
        return pl.pallas_call(
            functools.partial(
                correlate_kernel,
                width=width,
                tiles=count,
                partial=received is not None,
                scale=factor if last else None,
            ),
            out_shape=out_shape,
            grid=(1,),
            in_specs=in_specs,
            out_specs=out_spec,
            scratch_shapes=[pltpu.VMEM((16, height, LANES), f32)],
            input_output_aliases=aliases,
            compiler_params=pltpu.CompilerParams(vmem_limit_bytes=16 * 2**20),
            cost_estimate=pl.CostEstimate(flops=10**9, bytes_accessed=6 * 10**6, transcendentals=0),
            name="correlate",
        )(*operands)

    def fetch(step, g):
        own, same, core, cross = (outs[(i * strips + step) * len(groups) + g] for i in range(4))
        return own, send(same, to_same), send(core, to_core), send(cross, to_cross)

    image = None
    received = [None] * len(groups)
    for step in range(strips):
        for g in range(len(groups)):
            last = step == strips - 1
            result = correlate(fetch(step, g), received[g], last, image, g)
            if last:
                image = result
            else:
                received[g] = send(result, onward)
    return image


def solution(mesh):
    return jax.shard_map(
        shards,
        mesh=mesh,
        in_specs=(
            P(None, "freq", None, None, None),
            P(None, "freq", None, None, None),
            P("depth", None, None),
            P(),
            P(),
        ),
        out_specs=P("depth", None, "freq", None),
        check_vma=False,
    )
```

```python
import functools
import math

import jax
import jax.numpy as jnp
import ml_dtypes
import numpy as np
from jax import lax
from jax.experimental import pallas as pl
from jax.experimental.pallas import tpu as pltpu
from jax.sharding import PartitionSpec as P

LAG = 7
HALO = 8
LANES = 128
AXES = ("depth", "freq")
VMEM_BYTES = 24 * 2**20


RADIX = 4
BLOCKS_X = 2
BLOCKS_Y = 2


def residues(length):
    found = [np.arange(residue, length, RADIX) for residue in range(RADIX)]
    found[3] = found[3][::-1]
    return found


def residue_tables(length):
    position = np.arange(length, dtype=np.int64)
    product = position[:, None] * position[None, :] % length
    angles = product.astype(np.float32) * np.float32(2.0 * math.pi / length)
    factor = np.float32(1.0 / math.sqrt(length))
    cos, sin = np.cos(angles) * factor, np.sin(angles) * factor
    tables = []
    for residue in residues(length):
        c, s = (t[residue, : length // RADIX] for t in (cos, sin))
        tables.append(np.block([[c, s], [-s, c]]).astype(ml_dtypes.bfloat16))
    return np.stack(tables)


def wavenumbers_squared(length):
    position = np.arange(length)
    signed = np.where(position < length // 2, position, position - length)
    wave = signed.astype(np.float32) * np.float32(2.0 * math.pi / length)
    squared = wave * wave
    return np.concatenate([squared[residue] for residue in residues(length)[:3]])


def mix_forward(re, im):
    sum_re, dif_re = re[0] + re[2], re[0] - re[2]
    sum_im, dif_im = im[0] + im[2], im[0] - im[2]
    odd_re, gap_re = re[1] + re[3], re[1] - re[3]
    odd_im, gap_im = im[1] + im[3], im[1] - im[3]
    return (
        (sum_re + odd_re, sum_im + odd_im),
        (dif_re + gap_im, dif_im - gap_re),
        (sum_re - odd_re, sum_im - odd_im),
        (dif_re - gap_im, dif_im + gap_re),
    )


def mix_inverse(re, im):
    found = mix_forward(re, im)
    return found[0], found[3], found[2], found[1]


Q_MAX = 14.0


def fit(function, degree):
    cheb = np.polynomial.chebyshev.Chebyshev.interpolate(
        lambda t: function((t + 1.0) * Q_MAX / 2), degree
    )
    return [float(v) for v in np.polynomial.chebyshev.cheb2poly(cheb.coef)]


COS_FIT = fit(lambda q: np.cos(np.sqrt(q)), 7)
SINC_FIT = fit(lambda q: np.sinc(np.sqrt(q) / np.pi), 7)


def horner(coefficients, t):
    total = jnp.full_like(t, coefficients[-1])
    for value in coefficients[-2::-1]:
        total = total * t + value
    return total


def cos_sin(square, root):
    t = square * (2.0 / Q_MAX) - 1.0
    return horner(COS_FIT, t), horner(SINC_FIT, t) * root


def lookup(table_row, codes):
    rows = codes.shape[0]
    parts = []
    for tile in range(codes.shape[1] // LANES):
        index = codes[:, tile * LANES : (tile + 1) * LANES]
        source = jnp.broadcast_to(table_row, (rows, LANES))
        parts.append(jnp.take_along_axis(source, index, axis=1, mode="promise_in_bounds"))
    return parts


def chain_kernel(
    place, angular_ref, *refs, top, planes, begin, lead, closing, strips, width, tiles, groups, shots
):
    refs = list(refs)

    def take(count):
        return [refs.pop(0) for _ in range(count)]

    state = take(2 if top else 1)
    codes = [take(2) for _ in range(planes)]
    levels, left_x, right_x, left_y, right_y, wave_x, wave_y = take(7)
    phases, index, mid = refs[-3:]
    if closing:
        field, padded = refs[-5:-3]
        outs = refs[:-5]
    else:
        field = refs[0]
    rows_x, rows_y = field.shape[1], field.shape[2]
    part_x, part_y = rows_x // RADIX, rows_y // RADIX
    block_x, block_y = rows_x // BLOCKS_X, rows_y // BLOCKS_Y
    group, my_core, my_parity, spot = place[0], place[1], place[2], place[3]
    angular = angular_ref[0]
    f32, bf16 = jnp.float32, jnp.bfloat16

    if top:
        field[0:2] = state[0][my_core, 0]
        field[2:4] = state[1][my_core, 0]
    else:
        field[...] = state[0][...]

    def turned(kind, a, b, cos, sin):
        if kind == 0:
            return a * cos - b * sin, a * sin + b * cos
        return a * cos + b * sin, b * cos - a * sin

    def emit(target, parity):
        for s in range(strips):
            p = lax.rem(spot + (strips - 1 - s), strips)
            strip = jnp.where(p == 0, 0, jnp.where(p <= strips // 2, 2 * p - 1, 2 * (strips - p)))
            start = pl.multiple_of((2 * strip + parity) * width, 16)
            for g, (first, last) in enumerate(groups):
                for tile in range(first, last):
                    for part in range(4):
                        outs[(target * strips + s) * len(groups) + g][part, tile - first] = padded[
                            part, tile, pl.ds(start, width + 2 * HALO)
                        ]

    def step(t, carry):
        own = my_core == lax.rem(t + begin, shots)
        for j in range(planes):
            for flag, source in ((own, codes[j][0]), (jnp.logical_not(own), codes[j][1])):

                @pl.when((t == j) & flag)
                def _(source=source):
                    index[...] = source[...].astype(f32).astype(jnp.int32)

        def forward_x(i, total):
            cols = pl.ds(pl.multiple_of(i * block_y, block_y), block_y)
            for part in range(RADIX):
                at = index[part * part_x : (part + 1) * part_x, cols]
                value = functools.reduce(jnp.add, lookup(levels[0:1, :], at))
                total = total + jnp.sum(value.reshape(part_x // 8, 8, LANES), axis=0)
            for kind in range(2):
                re, im = (
                    [field[2 * kind + j, q * part_x : (q + 1) * part_x, cols] for q in range(RADIX)]
                    for j in range(2)
                )
                for r, mixed in enumerate(mix_forward(re, im)):
                    mixed = jnp.concatenate(mixed, axis=0)
                    out = jnp.dot(left_x[r], mixed, preferred_element_type=f32).astype(bf16)
                    mid[2 * kind : 2 * kind + 2, r * part_x : (r + 1) * part_x, cols] = (
                        out.reshape(2, part_x, block_y)
                    )
            return total

        total = lax.fori_loop(0, BLOCKS_Y, forward_x, jnp.zeros((8, LANES), f32), unroll=True)
        base = jnp.sum(total) / (rows_x * rows_y)
        angle = angular * (levels[0:1, :] - base)
        screen = cos_sin(angle * angle, angle)
        reach = angular * base
        reach = reach * reach

        def phase(i, carry):
            rows = pl.ds(pl.multiple_of(i * part_x, part_x), part_x)
            q = reach - wave_x[rows, :] - wave_y[0:1, :]
            root = jnp.sqrt(jnp.abs(q))
            cos, sin = cos_sin(q, root)
            phases[0, rows] = jnp.where(q > 0.0, cos, jnp.exp(-root))
            phases[1, rows] = jnp.where(q > 0.0, sin, 0.0)
            return carry

        lax.fori_loop(0, 3, phase, 0)

        def along_y(i, carry):
            rows = slice(i * part_x, (i + 1) * part_x)
            same = slice((1 if i == 3 else i) * part_x, (1 if i == 3 else i) * part_x + part_x)
            lanes = [slice(q * part_y, (q + 1) * part_y) for q in range(RADIX)]
            re, im = (
                [
                    jnp.concatenate([mid[j, rows, at], mid[2 + j, rows, at]], axis=0)
                    for at in lanes
                ]
                for j in range(2)
            )
            back = []
            for r, mixed in enumerate(mix_forward(re, im)):
                mixed = jnp.concatenate(mixed, axis=1)
                spectrum = jnp.dot(mixed, right_y[r], preferred_element_type=f32)
                at = lanes[1 if r == 3 else r]
                phase_re, phase_im = phases[0, same, at], phases[1, same, at]
                pieces = []
                for kind in range(2):
                    part = spectrum[kind * part_x : (kind + 1) * part_x]
                    new = turned(kind, part[:, :part_y], part[:, part_y:], phase_re, phase_im)
                    pieces.append(jnp.concatenate(new, axis=1).astype(bf16))
                shifted = jnp.concatenate(pieces, axis=0)
                back.append(jnp.dot(shifted, left_y[r], preferred_element_type=f32))
            back_re = [value[:, :part_y] for value in back]
            back_im = [value[:, part_y:] for value in back]
            for at, mixed in zip(lanes, mix_inverse(back_re, back_im)):
                for j in range(2):
                    value = mixed[j].astype(bf16)
                    for kind in range(2):
                        mid[2 * kind + j, rows, at] = value[kind * part_x : (kind + 1) * part_x]
            return carry

        [along_y(i, 0) for i in range(RADIX)]

        def inverse_x(i, carry):
            cols = pl.ds(pl.multiple_of(i * block_y, block_y), block_y)
            turn = []
            for part in range(RADIX):
                at = index[part * part_x : (part + 1) * part_x, cols]
                turn.append([jnp.concatenate(lookup(table, at), axis=1) for table in screen])
            for kind in range(2):
                back = [
                    jnp.dot(
                        right_x[r],
                        mid[2 * kind : 2 * kind + 2, r * part_x : (r + 1) * part_x, cols].reshape(
                            2 * part_x, block_y
                        ),
                        preferred_element_type=f32,
                    )
                    for r in range(RADIX)
                ]
                back_re = [value[:part_x] for value in back]
                back_im = [value[part_x:] for value in back]
                done = [
                    turned(kind, a, b, *turn[part])
                    for part, (a, b) in enumerate(mix_inverse(back_re, back_im))
                ]
                for j in range(2):
                    for part in range(RADIX):
                        at = slice(part * part_x, (part + 1) * part_x)
                        field[2 * kind + j, at, cols] = done[part][j].astype(bf16)
                    if closing:
                        edge = jnp.zeros((HALO, block_y), f32)
                        whole = jnp.concatenate([edge, *(d[j] for d in done), edge], axis=0)
                        whole = whole.astype(bf16)
                        for k in range(block_y // LANES):
                            padded[2 * kind + j, i * (block_y // LANES) + k] = whole[
                                :, k * LANES : (k + 1) * LANES
                            ]
            return carry

        lax.fori_loop(0, BLOCKS_Y, inverse_x, 0, unroll=True)
        if not closing:
            return carry

        @pl.when((t >= lead) & own)
        def _():
            emit(0, my_parity)
            emit(1, 1 - my_parity)

        @pl.when((t >= lead) & jnp.logical_not(own))
        def _():
            emit(2, my_parity)
            emit(3, 1 - my_parity)

        return carry

    lax.fori_loop(jnp.where(group == 0, lead, 0), planes, step, 0)


def correlate_kernel(*refs, width, tiles, partial, scale):
    fields, refs = refs[:4], refs[4:]
    received = None
    if partial:
        received, refs = refs[0], refs[1:]
    out, wide = refs[-2], refs[-1]
    for tile in range(tiles):
        lanes = slice(tile * LANES, (tile + 1) * LANES)
        for m in range(4):
            for part in range(4):
                wide[m * 4 + part] = fields[m][part, tile].astype(jnp.float32)
        for lag in range(2 * LAG + 1):
            shift = lag - LAG
            total = None
            for m in range(4):
                for part in range(2):
                    term = (
                        wide[m * 4 + part, HALO - shift : HALO - shift + width]
                        * wide[m * 4 + 2 + part, HALO + shift : HALO + shift + width]
                    )
                    total = term if total is None else total + term
            if received is not None:
                total = total + received[lag, tile].astype(jnp.float32)
            if scale is not None:
                out[0, lag, :, lanes] = total * scale
            else:
                out[lag, tile] = total.astype(out.dtype)


def window_kernel(place, anchors, mine, other, out_mine, out_other):
    del place, anchors
    out_mine[...] = mine[0].astype(jnp.float32).astype(out_mine.dtype)
    out_other[...] = other[0].astype(jnp.float32).astype(out_other.dtype)


def pinned(x):
    return pltpu.with_memory_space_constraint(x, pltpu.VMEM)


def chain(
    place, angular, table, *, tops=None, state=None, codes, begin, lead, closing, strips, width, groups, shots
):
    rows_x, rows_y = (tops[0] if tops else state).shape[-2:]
    tiles = rows_y // LANES
    bf16, f32 = jnp.bfloat16, jnp.float32
    tables_x, tables_y = residue_tables(rows_x), residue_tables(rows_y)
    left_x, right_x = jnp.asarray(tables_x), jnp.asarray(np.swapaxes(tables_x, 1, 2))
    left_y, right_y = (left_x, right_x) if rows_x == rows_y else (
        jnp.asarray(tables_y), jnp.asarray(np.swapaxes(tables_y, 1, 2))
    )
    wave_x = wavenumbers_squared(rows_x)[:, None]
    wave_y = wavenumbers_squared(rows_y)[None]
    height = width + 2 * HALO
    vmem = pl.BlockSpec(memory_space=pltpu.VMEM)
    operands = list(tops) if tops else [state]
    in_specs = []
    for pair in codes:
        operands += list(pair)
    operands += [
        jnp.pad(table, (0, LANES - table.shape[0]))[None],
        left_x, right_x, left_y, right_y, jnp.asarray(wave_x), jnp.asarray(wave_y),
    ]
    in_specs += [vmem] * (len(operands) - len(in_specs))
    whole = (4, rows_x, rows_y)
    scratch = [
        pltpu.VMEM((2, 3 * rows_x // RADIX, 3 * rows_y // RADIX), f32),
        pltpu.VMEM((rows_x, rows_y), jnp.int32),
        pltpu.VMEM(whole, bf16),
    ]
    if closing:
        out_shape = [
            pltpu.VMEM((4, last - first, height, LANES), bf16)
            for _ in range(4 * strips)
            for first, last in groups
        ]
        scratch = [
            pltpu.VMEM(whole, bf16),
            pltpu.VMEM((4, tiles, rows_x + 2 * HALO, LANES), bf16),
        ] + scratch
    else:
        out_shape = [pltpu.VMEM(whole, bf16)]
    return pl.pallas_call(
        functools.partial(
            chain_kernel, top=bool(tops), planes=len(codes), begin=begin, lead=lead, closing=closing,
            strips=strips, width=width, tiles=tiles, groups=groups, shots=shots,
        ),
        out_shape=out_shape,
        grid_spec=pltpu.PrefetchScalarGridSpec(
            num_scalar_prefetch=2,
            grid=(1,),
            in_specs=in_specs,
            out_specs=[vmem] * len(out_shape),
            scratch_shapes=scratch,
        ),
        compiler_params=pltpu.CompilerParams(vmem_limit_bytes=VMEM_BYTES),
        cost_estimate=pl.CostEstimate(
            flops=9 * 10**9 * len(codes), bytes_accessed=10**7, transcendentals=0
        ),
        name="chain",
    )(place, angular, *(pinned(x) for x in operands))


def windows(place, anchors, slowness_codes, rows_x, rows_y):
    steps = 4
    rows = rows_x // steps

    def block(flip):
        def index(i, place, anchors):
            shot = jnp.abs(place[1] - flip)
            return (0, anchors[shot, 0] // rows + i, anchors[shot, 1] // rows_y)

        return pl.BlockSpec((1, rows, rows_y), index)

    code_spec = pl.BlockSpec((rows, rows_y), lambda i, place, anchors: (i, 0))
    return pl.pallas_call(
        window_kernel,
        out_shape=[pltpu.VMEM((rows_x, rows_y), jnp.bfloat16)] * 2,
        grid_spec=pltpu.PrefetchScalarGridSpec(
            num_scalar_prefetch=2,
            grid=(steps,),
            in_specs=[block(0), block(1)],
            out_specs=[code_spec, code_spec],
        ),
        name="windows",
    )(place, anchors, slowness_codes, slowness_codes)


def shards(source_top, receiver_top, slowness_codes, slowness_table, anchors):
    shots, _, _, rows_x, rows_y = source_top.shape
    freq_count = lax.axis_size("freq")
    depth_count = lax.axis_size("depth")
    strips = freq_count // 2
    width = rows_x // freq_count
    lags = 2 * LAG + 1
    tiles = rows_y // LANES
    groups = [(0, tiles // 2), (tiles // 2, tiles)]
    factor = 1.0 / math.sqrt(2.0 * shots * freq_count)
    depth_index = lax.axis_index("depth")
    freq_index = lax.axis_index("freq")
    my_core = depth_index % shots
    group = depth_index // shots
    bf16, f32 = jnp.bfloat16, jnp.float32

    def number(group_at, core_at, strip_at, parity_at):
        return (group_at * shots + core_at) * freq_count + strip_at * 2 + parity_at

    def pairs(move):
        found = []
        for g in range(depth_count // shots):
            for c in range(shots):
                for z in range(strips):
                    for x in range(2):
                        to = move(g, c, z, x)
                        if to is not None:
                            found.append((number(g, c, z, x), number(*to)))
        return found

    def send(value, move):
        return lax.ppermute(value, AXES, pairs(move))

    def to_core(g, c, z, x):
        return (g, 1 - c, z, x)

    def to_same(g, c, z, x):
        return (g, c, z, 1 - x)

    def to_cross(g, c, z, x):
        return (g, 1 - c, z, 1 - x)

    def up(core):
        return lambda g, c, z, x: (1, c, z, x) if g == 0 and c == core else None

    ring = [0] + list(range(1, strips, 2)) + list(range(2, strips, 2))[::-1]
    spots = {z: p for p, z in enumerate(ring)}

    def onward(g, c, z, x):
        return (g, c, ring[(spots[z] + 1) % strips], x)

    my_strip = freq_index // 2
    spot = jnp.where(
        my_strip == 0,
        0,
        jnp.where(my_strip % 2 == 1, (my_strip + 1) // 2, strips - my_strip // 2),
    )
    place = jnp.stack([group, my_core, freq_index % 2, spot]).astype(jnp.int32)

    mine, other = windows(place, anchors, slowness_codes, rows_x, rows_y)
    from_core = send(other, to_core)
    near = (mine, from_core)
    far = [(send(mine, up(0)), send(from_core, up(1)))]
    mine_later, from_core_later = lax.optimization_barrier((mine, from_core))
    far.append((send(mine_later, up(1)), send(from_core_later, up(0))))

    angular = (math.pi * (0.45 + 0.5 * (freq_index.astype(f32) + 0.5) / freq_count))[None]
    common = dict(strips=strips, width=width, groups=groups, shots=shots)
    (state,) = chain(
        place, angular, slowness_table, tops=(source_top, receiver_top), codes=far[:1], begin=0, lead=1,
        closing=False, **common,
    )
    outs = chain(
        place, angular, slowness_table, state=state, codes=far[1:] + [near] * shots, begin=1, lead=shots - 1,

        closing=True, **common,
    )
    height = width + 2 * HALO

    def correlate(fields, received, last, buffer, g):
        first, end = groups[g]
        count = end - first
        operands = [pinned(x) for x in fields]
        field_spec = image_spec = pl.BlockSpec(memory_space=pltpu.VMEM)
        in_specs = [field_spec] * 4
        if received is not None:
            in_specs.append(image_spec)
            operands.append(pinned(received))
        aliases = {}
        if last:
            out_shape = jax.ShapeDtypeStruct((1, lags, width, rows_y), f32)
            out_spec = pl.BlockSpec(
                (1, lags, width, count * LANES), lambda i: (0, 0, 0, first // count)
            )
            if buffer is not None:
                in_specs.append(pl.BlockSpec(memory_space=pl.ANY))
                aliases = {len(operands): 0}
                operands.append(buffer)
        else:
            out_shape = pltpu.VMEM((lags, count, width, LANES), bf16)
            out_spec = image_spec
        return pl.pallas_call(
            functools.partial(
                correlate_kernel,
                width=width,
                tiles=count,
                partial=received is not None,
                scale=factor if last else None,
            ),
            out_shape=out_shape,
            grid=(1,),
            in_specs=in_specs,
            out_specs=out_spec,
            scratch_shapes=[pltpu.VMEM((16, height, LANES), f32)],
            input_output_aliases=aliases,
            compiler_params=pltpu.CompilerParams(vmem_limit_bytes=16 * 2**20),
            cost_estimate=pl.CostEstimate(flops=10**9, bytes_accessed=6 * 10**6, transcendentals=0),
            name="correlate",
        )(*operands)

    def fetch(step, g):
        own, same, core, cross = (outs[(i * strips + step) * len(groups) + g] for i in range(4))
        return own, send(same, to_same), send(core, to_core), send(cross, to_cross)

    image = None
    received = [None] * len(groups)
    for step in range(strips):
        for g in range(len(groups)):
            last = step == strips - 1
            result = correlate(fetch(step, g), received[g], last, image, g)
            if last:
                image = result
            else:
                received[g] = send(result, onward)
    return image


def solution(mesh):
    return jax.shard_map(
        shards,
        mesh=mesh,
        in_specs=(
            P(None, "freq", None, None, None),
            P(None, "freq", None, None, None),
            P("depth", None, None),
            P(),
            P(),
        ),
        out_specs=P("depth", None, "freq", None),
        check_vma=False,
    )
```

```python
import functools
import math

import jax
import jax.numpy as jnp
import ml_dtypes
import numpy as np
from jax import lax
from jax.experimental import pallas as pl
from jax.experimental.pallas import tpu as pltpu
from jax.sharding import PartitionSpec as P

LAG = 7
HALO = 8
LANES = 128
AXES = ("depth", "freq")
VMEM_BYTES = 24 * 2**20


RADIX = 4
BLOCKS_X = 2
BLOCKS_Y = 2


def residues(length):
    found = [np.arange(residue, length, RADIX) for residue in range(RADIX)]
    found[3] = found[3][::-1]
    return found


def residue_tables(length):
    position = np.arange(length, dtype=np.int64)
    product = position[:, None] * position[None, :] % length
    angles = product.astype(np.float32) * np.float32(2.0 * math.pi / length)
    factor = np.float32(1.0 / math.sqrt(length))
    cos, sin = np.cos(angles) * factor, np.sin(angles) * factor
    tables = []
    for residue in residues(length):
        c, s = (t[residue, : length // RADIX] for t in (cos, sin))
        tables.append(np.block([[c, s], [-s, c]]).astype(ml_dtypes.bfloat16))
    return np.stack(tables)


def wavenumbers_squared(length):
    position = np.arange(length)
    signed = np.where(position < length // 2, position, position - length)
    wave = signed.astype(np.float32) * np.float32(2.0 * math.pi / length)
    squared = wave * wave
    return np.concatenate([squared[residue] for residue in residues(length)[:3]])


def mix_forward(re, im):
    sum_re, dif_re = re[0] + re[2], re[0] - re[2]
    sum_im, dif_im = im[0] + im[2], im[0] - im[2]
    odd_re, gap_re = re[1] + re[3], re[1] - re[3]
    odd_im, gap_im = im[1] + im[3], im[1] - im[3]
    return (
        (sum_re + odd_re, sum_im + odd_im),
        (dif_re + gap_im, dif_im - gap_re),
        (sum_re - odd_re, sum_im - odd_im),
        (dif_re - gap_im, dif_im + gap_re),
    )


def mix_inverse(re, im):
    found = mix_forward(re, im)
    return found[0], found[3], found[2], found[1]


Q_MAX = 14.0


def fit(function, degree):
    cheb = np.polynomial.chebyshev.Chebyshev.interpolate(
        lambda t: function((t + 1.0) * Q_MAX / 2), degree
    )
    return [float(v) for v in np.polynomial.chebyshev.cheb2poly(cheb.coef)]


COS_FIT = fit(lambda q: np.cos(np.sqrt(q)), 7)
SINC_FIT = fit(lambda q: np.sinc(np.sqrt(q) / np.pi), 7)


def horner(coefficients, t):
    total = jnp.full_like(t, coefficients[-1])
    for value in coefficients[-2::-1]:
        total = total * t + value
    return total


def cos_sin(square, root):
    t = square * (2.0 / Q_MAX) - 1.0
    return horner(COS_FIT, t), horner(SINC_FIT, t) * root


def lookup(table_row, codes):
    rows = codes.shape[0]
    parts = []
    for tile in range(codes.shape[1] // LANES):
        index = codes[:, tile * LANES : (tile + 1) * LANES]
        source = jnp.broadcast_to(table_row, (rows, LANES))
        parts.append(jnp.take_along_axis(source, index, axis=1, mode="promise_in_bounds"))
    return parts


def turned(kind, a, b, cos, sin):
    if kind == 0:
        return a * cos - b * sin, a * sin + b * cos
    return a * cos + b * sin, b * cos - a * sin


def extent(ref):
    rows_x, rows_y = ref.shape[1], ref.shape[2]
    return rows_x // RADIX, rows_y // RADIX, rows_y // BLOCKS_Y


def forward_x(field, mid, left_x):
    part_x, _, block_y = extent(field)
    for i in range(BLOCKS_Y):
        cols = slice(i * block_y, (i + 1) * block_y)
        for kind in range(2):
            re, im = (
                [field[2 * kind + j, q * part_x : (q + 1) * part_x, cols] for q in range(RADIX)]
                for j in range(2)
            )
            for r, mixed in enumerate(mix_forward(re, im)):
                mixed = jnp.concatenate(mixed, axis=0)
                out = jnp.dot(left_x[r], mixed, preferred_element_type=jnp.float32)
                mid[2 * kind : 2 * kind + 2, r * part_x : (r + 1) * part_x, cols] = out.astype(
                    jnp.bfloat16
                ).reshape(2, part_x, block_y)


def fill_phases(angular, base, wave_x, wave_y, phases):
    reach = angular * base
    reach = reach * reach
    part = wave_x.shape[0] // 3

    def block(i, carry):
        rows = pl.ds(pl.multiple_of(i * part, part), part)
        q = reach - wave_x[rows, :] - wave_y[0:1, :]
        root = jnp.sqrt(jnp.abs(q))
        cos, sin = cos_sin(q, root)
        phases[0, rows] = jnp.where(q > 0.0, cos, jnp.exp(-root))
        phases[1, rows] = jnp.where(q > 0.0, sin, 0.0)
        return carry

    lax.fori_loop(0, 3, block, 0)


def along_y(mid, phases, left_y, right_y):
    part_x, part_y, _ = extent(mid)
    lanes = [slice(q * part_y, (q + 1) * part_y) for q in range(RADIX)]
    for i in range(RADIX):
        rows = slice(i * part_x, (i + 1) * part_x)
        same = slice(part_x, 2 * part_x) if i == 3 else rows
        re, im = (
            [jnp.concatenate([mid[j, rows, at], mid[2 + j, rows, at]], axis=0) for at in lanes]
            for j in range(2)
        )
        back = []
        for r, mixed in enumerate(mix_forward(re, im)):
            mixed = jnp.concatenate(mixed, axis=1)
            spectrum = jnp.dot(mixed, right_y[r], preferred_element_type=jnp.float32)
            at = lanes[1 if r == 3 else r]
            phase_re, phase_im = phases[0, same, at], phases[1, same, at]
            pieces = []
            for kind in range(2):
                part = spectrum[kind * part_x : (kind + 1) * part_x]
                new = turned(kind, part[:, :part_y], part[:, part_y:], phase_re, phase_im)
                pieces.append(jnp.concatenate(new, axis=1).astype(jnp.bfloat16))
            shifted = jnp.concatenate(pieces, axis=0)
            back.append(jnp.dot(shifted, left_y[r], preferred_element_type=jnp.float32))
        back_re = [value[:, :part_y] for value in back]
        back_im = [value[:, part_y:] for value in back]
        for at, mixed in zip(lanes, mix_inverse(back_re, back_im)):
            for j in range(2):
                value = mixed[j].astype(jnp.bfloat16)
                for kind in range(2):
                    mid[2 * kind + j, rows, at] = value[kind * part_x : (kind + 1) * part_x]


def inverse_x(mid, right_x, sink):
    part_x, _, block_y = extent(mid)
    for i in range(BLOCKS_Y):
        cols = slice(i * block_y, (i + 1) * block_y)
        for kind in range(2):
            back = [
                jnp.dot(
                    right_x[r],
                    mid[2 * kind : 2 * kind + 2, r * part_x : (r + 1) * part_x, cols].reshape(
                        2 * part_x, block_y
                    ),
                    preferred_element_type=jnp.float32,
                )
                for r in range(RADIX)
            ]
            back_re = [value[:part_x] for value in back]
            back_im = [value[part_x:] for value in back]
            sink(i, cols, kind, mix_inverse(back_re, back_im))


def screen_tables(angular, base, levels):
    angle = angular * (levels[0:1, :] - base)
    return cos_sin(angle * angle, angle)


def fill_index(index, pair, flag):
    for value, source in ((flag, pair[0]), (jnp.logical_not(flag), pair[1])):

        @pl.when(value)
        def _(source=source):
            index[...] = source[...].astype(jnp.float32).astype(jnp.int32)


def screens_of(tables, index, rows, cols):
    return [jnp.concatenate(lookup(table, index[rows, cols]), axis=1) for table in tables]


def put_screened(tables, index, field, padded=None):
    part_x, _, block_y = extent(field)
    kept = {}

    def sink(i, cols, kind, parts):
        if i not in kept:
            kept.clear()
            kept[i] = [
                screens_of(tables, index, slice(p * part_x, (p + 1) * part_x), cols)
                for p in range(RADIX)
            ]
        done = [turned(kind, a, b, *kept[i][p]) for p, (a, b) in enumerate(parts)]
        for j in range(2):
            for p in range(RADIX):
                at = slice(p * part_x, (p + 1) * part_x)
                field[2 * kind + j, at, cols] = done[p][j].astype(jnp.bfloat16)
            if padded is not None:
                edge = jnp.zeros((HALO, block_y), jnp.float32)
                whole = jnp.concatenate([edge, *(d[j] for d in done), edge], axis=0)
                whole = whole.astype(jnp.bfloat16)
                for k in range(block_y // LANES):
                    padded[2 * kind + j, i * (block_y // LANES) + k] = whole[
                        :, k * LANES : (k + 1) * LANES
                    ]

    return sink


def prepare_kernel(place, angular_ref, source, receiver, mine, from_core, levels, *refs, shots):
    count = (len(refs) - 7) // 2
    tables, refs = refs[:count], refs[count:]
    wave_x, wave_y, top, mid, means, phases = refs[:6]
    kept, index = refs[6:-1], refs[-1]
    angular, my_core = angular_ref[0], place[1]
    for table, copy in zip(tables, kept):
        copy[...] = table[...]
    top[0:2] = source[0, 0]
    top[2:4] = receiver[0, 0]
    rows_x, rows_y = index.shape
    for p in range(shots):
        fill_index(index, (mine, from_core), my_core == p)
        if p == 0:
            forward_x(top, mid, tables[0])
        value = functools.reduce(jnp.add, lookup(levels[0:1, :], index[...]))
        base = jnp.sum(jnp.sum(value.reshape(rows_x // 8, 8, LANES), axis=0)) / (rows_x * rows_y)
        means[p : p + 1, :] = jnp.full((1, LANES), base, jnp.float32)
        fill_phases(angular, base, wave_x, wave_y, phases.at[p])


def lead_kernel(
    place, angular_ref, first, far_a, far_b, means, levels, left_x, right_x, left_y, right_y,
    wave_x, wave_y, before, mid, field, index, phases,
):
    angular, my_core = angular_ref[0], place[1]

    def put_plain(i, cols, kind, parts):
        part_x = extent(field)[0]
        for p, values in enumerate(parts):
            for j in range(2):
                before[2 * kind + j, p * part_x : (p + 1) * part_x, cols] = values[j]

    @pl.when(place[0] > 0)
    def _():
        fill_phases(angular, means[0:1, 0:1], wave_x, wave_y, phases)
        mid[...] = first[...]
        along_y(mid, phases, left_y, right_y)
        fill_index(index, (far_a, far_b), my_core == 0)
        tables = screen_tables(angular, means[0:1, 0:1], levels)
        inverse_x(mid, right_x, put_screened(tables, index, field))
        forward_x(field, mid, left_x)
        fill_phases(angular, means[1:2, 0:1], wave_x, wave_y, phases)
        along_y(mid, phases, left_y, right_y)
        inverse_x(mid, right_x, put_plain)


def planes_kernel(place, angular_ref, *refs, shots, strips, width, groups, later):
    refs = list(refs)
    top, before, far_a, far_b, far_means, near_a, near_b, means, phases, levels = refs[:10]
    left_x, right_x, left_y, right_y = refs[10:14]
    outs = refs[14:-4]
    field, mid, padded, index = refs[-4:]
    angular, my_core, parity, spot = angular_ref[0], place[1], place[2], place[3]

    @pl.when(place[0] == 0)
    def _():
        field[...] = top[...]

    @pl.when(place[0] > 0)
    def _():
        fill_index(index, (far_a, far_b), my_core == 1)
        tables = screen_tables(angular, far_means[1:2, 0:1], levels)
        block = 128

        def part(i, carry):
            rows = pl.ds(pl.multiple_of(i * block, block), block)
            cos, sin = screens_of(tables, index, rows, slice(None))
            for kind in range(2):
                new = turned(kind, before[2 * kind, rows], before[2 * kind + 1, rows], cos, sin)
                for j in range(2):
                    field[2 * kind + j, rows] = new[j].astype(jnp.bfloat16)
            return carry

        lax.fori_loop(0, index.shape[0] // block, part, 0)

    def emit(target, to):
        for s in range(strips):
            p = lax.rem(spot + (strips - 1 - s), strips)
            strip = jnp.where(p == 0, 0, jnp.where(p <= strips // 2, 2 * p - 1, 2 * (strips - p)))
            start = pl.multiple_of((2 * strip + to) * width, 16)
            for n, (first, last) in enumerate(groups if s == 0 else later):
                at = n if s == 0 else len(groups) + (s - 1) * len(later) + n
                out = outs[target * (len(groups) + (strips - 1) * len(later)) + at]
                for tile in range(first, last):
                    for part in range(4):
                        out[part, tile - first] = padded[part, tile, pl.ds(start, width + 2 * HALO)]

    for plane in range(shots):
        forward_x(field, mid, left_x)
        fill_index(index, (near_a, near_b), my_core == plane)
        along_y(mid, phases.at[plane], left_y, right_y)
        tables = screen_tables(angular, means[plane : plane + 1, 0:1], levels)
        inverse_x(mid, right_x, put_screened(tables, index, field, padded))

        @pl.when(my_core == plane)
        def _():
            emit(0, parity)
            emit(1, 1 - parity)

        @pl.when(my_core != plane)
        def _():
            emit(2, parity)
            emit(3, 1 - parity)


def correlate_kernel(*refs, width, begin, tiles, partial, scale):
    fields, out, wide = refs[:4], refs[-2], refs[-1]
    for tile in range(tiles):
        lanes = slice(tile * LANES, (tile + 1) * LANES)
        for m in range(4):
            for part in range(4):
                wide[m * 4 + part] = fields[m][part, begin + tile].astype(jnp.float32)
        for lag in range(2 * LAG + 1):
            shift = lag - LAG
            total = None
            for m in range(4):
                for part in range(2):
                    term = (
                        wide[m * 4 + part, HALO - shift : HALO - shift + width]
                        * wide[m * 4 + 2 + part, HALO + shift : HALO + shift + width]
                    )
                    total = term if total is None else total + term
            if partial:
                total = total + refs[4][lag, tile].astype(jnp.float32)
            if scale is not None:
                out[0, lag, :, lanes] = total * scale
            else:
                out[lag, tile] = total.astype(out.dtype)


def window_kernel(place, anchors, mine, other, out_mine, out_other):
    del place, anchors
    out_mine[...] = mine[0].astype(jnp.float32).astype(out_mine.dtype)
    out_other[...] = other[0].astype(jnp.float32).astype(out_other.dtype)


def pinned(x):
    return pltpu.with_memory_space_constraint(x, pltpu.VMEM)


def unpinned(x):
    return pltpu.with_memory_space_constraint(x, pltpu.HBM)


VMEM_SPEC = pl.BlockSpec(memory_space=pltpu.VMEM)


def call(kernel, name, scalars, operands, outs, scratch, flops):
    return pl.pallas_call(
        kernel,
        out_shape=[pltpu.VMEM(shape, dtype) for shape, dtype in outs],
        grid_spec=pltpu.PrefetchScalarGridSpec(
            num_scalar_prefetch=len(scalars),
            grid=(1,),
            in_specs=[VMEM_SPEC] * len(operands),
            out_specs=[VMEM_SPEC] * len(outs),
            scratch_shapes=scratch,
        ),
        compiler_params=pltpu.CompilerParams(vmem_limit_bytes=VMEM_BYTES),
        cost_estimate=pl.CostEstimate(flops=flops, bytes_accessed=10**6, transcendentals=0),
        name=name,
    )(*scalars, *(pinned(x) for x in operands))


def windows(place, anchors, slowness_codes, rows_x, rows_y):
    steps = 4
    rows = rows_x // steps

    def block(flip):
        def index(i, place, anchors):
            shot = jnp.abs(place[1] - flip)
            return (0, anchors[shot, 0] // rows + i, anchors[shot, 1] // rows_y)

        return pl.BlockSpec((1, rows, rows_y), index)

    code_spec = pl.BlockSpec((rows, rows_y), lambda i, place, anchors: (i, 0))
    return pl.pallas_call(
        window_kernel,
        out_shape=[
            pltpu.VMEM((rows_x, rows_y), jnp.bfloat16),
            pltpu.HBM((rows_x, rows_y), jnp.bfloat16),
        ],
        grid_spec=pltpu.PrefetchScalarGridSpec(
            num_scalar_prefetch=2,
            grid=(steps,),
            in_specs=[block(0), block(1)],
            out_specs=[code_spec, code_spec],
        ),
        name="windows",
    )(place, anchors, slowness_codes, slowness_codes)


def shards(source_top, receiver_top, slowness_codes, slowness_table, anchors):
    shots, _, _, rows_x, rows_y = source_top.shape
    freq_count = lax.axis_size("freq")
    depth_count = lax.axis_size("depth")
    strips = freq_count // 2
    width = rows_x // freq_count
    height = width + 2 * HALO
    lags = 2 * LAG + 1
    tiles = rows_y // LANES
    groups = [(0, tiles // 2), (tiles // 2, tiles)]
    later = groups
    factor = 1.0 / math.sqrt(2.0 * shots * freq_count)
    depth_index = lax.axis_index("depth")
    freq_index = lax.axis_index("freq")
    my_core = depth_index % shots
    group = depth_index // shots
    bf16, f32 = jnp.bfloat16, jnp.float32

    def number(group_at, core_at, strip_at, parity_at):
        return (group_at * shots + core_at) * freq_count + strip_at * 2 + parity_at

    def pairs(move, core):
        found = []
        for g in range(depth_count // shots):
            for c in range(shots):
                for z in range(strips):
                    for x in range(2):
                        to = move(g, c, z, x)
                        if core in (None, c) and to is not None:
                            found.append((number(g, c, z, x), number(*to)))
        return found

    def send(value, move, core=None):
        return lax.ppermute(value, AXES, pairs(move, core))

    def to_core(g, c, z, x):
        return (g, 1 - c, z, x)

    def to_same(g, c, z, x):
        return (g, c, z, 1 - x)

    def to_cross(g, c, z, x):
        return (g, 1 - c, z, 1 - x)

    def up(g, c, z, x):
        return (1, c, z, x) if g == 0 else None

    ring = [0] + list(range(1, strips, 2)) + list(range(2, strips, 2))[::-1]
    spots = {z: p for p, z in enumerate(ring)}

    def onward(g, c, z, x):
        return (g, c, ring[(spots[z] + 1) % strips], x)

    my_strip = freq_index // 2
    spot = jnp.where(
        my_strip == 0,
        0,
        jnp.where(my_strip % 2 == 1, (my_strip + 1) // 2, strips - my_strip // 2),
    )
    place = jnp.stack([group, my_core, freq_index % 2, spot]).astype(jnp.int32)
    angular = (math.pi * (0.45 + 0.5 * (freq_index.astype(f32) + 0.5) / freq_count))[None]
    scalars = (place, angular)

    mine, other = windows(place, anchors, slowness_codes, rows_x, rows_y)
    from_core = send(other, to_core)
    near = (mine, from_core)
    far_first = (send(mine, up, 0), send(from_core, up, 1))

    levels = jnp.pad(slowness_table, (0, LANES - slowness_table.shape[0]))[None]
    tables = []
    for length in (rows_x,) if rows_x == rows_y else (rows_x, rows_y):
        left = residue_tables(length)
        tables += [jnp.asarray(left), jnp.asarray(np.swapaxes(left, 1, 2))]
    wave_x = jnp.asarray(wavenumbers_squared(rows_x)[:, None])
    wave_y = jnp.asarray(wavenumbers_squared(rows_y)[None])
    whole = (4, rows_x, rows_y)
    phase_shape = (2, wave_x.shape[0], wave_y.shape[1])
    index_scratch = pltpu.VMEM((rows_x, rows_y), jnp.int32)
    top_spec = pl.BlockSpec(
        (1, 1, 2, rows_x, rows_y), lambda i, place, angular: (place[1], 0, 0, 0, 0)
    )
    prepared = pl.pallas_call(
        functools.partial(prepare_kernel, shots=shots),
        out_shape=[
            pltpu.VMEM(whole, bf16),
            pltpu.VMEM(whole, bf16),
            pltpu.VMEM((8, LANES), f32),
            pltpu.VMEM((shots, *phase_shape), f32),
            *(pltpu.VMEM(t.shape, t.dtype) for t in tables),
        ],
        grid_spec=pltpu.PrefetchScalarGridSpec(
            num_scalar_prefetch=2,
            grid=(1,),
            in_specs=[top_spec] * 2 + [VMEM_SPEC] * (5 + len(tables)),
            out_specs=[VMEM_SPEC] * (4 + len(tables)),
            scratch_shapes=[index_scratch],
        ),
        compiler_params=pltpu.CompilerParams(vmem_limit_bytes=VMEM_BYTES),
        cost_estimate=pl.CostEstimate(flops=4 * 10**9, bytes_accessed=10**6, transcendentals=0),
        name="prepare",
    )(
        *scalars, unpinned(source_top), unpinned(receiver_top), pinned(mine), pinned(from_core),
        levels, *(unpinned(t) for t in tables), wave_x, wave_y,
    )
    top, first, means, phases, *tables = prepared
    tables = list(tables) if len(tables) == 4 else list(tables) * 2

    far_means = send(means, up)
    mine_later, from_core_later, _ = lax.optimization_barrier((mine, from_core, means))
    far_second = (send(mine_later, up, 1), send(from_core_later, up, 0))

    (before,) = call(
        lead_kernel,
        "lead",
        scalars,
        [first, *far_first, far_means, levels, *tables, wave_x, wave_y],
        [(whole, f32)],
        [pltpu.VMEM(whole, bf16), pltpu.VMEM(whole, bf16), index_scratch, pltpu.VMEM(phase_shape, f32)],
        15 * 10**9,
    )
    sizes = [end - begin for begin, end in groups]
    sizes += [end - begin for begin, end in later] * (strips - 1)
    pieces = call(
        functools.partial(
            planes_kernel, shots=shots, strips=strips, width=width, groups=groups, later=later
        ),
        "planes",
        scalars,
        [top, before, *far_second, far_means, *near, means, phases, levels, *tables],
        [((4, size, height, LANES), bf16) for _ in range(4) for size in sizes],
        [
            pltpu.VMEM(whole, bf16),
            pltpu.VMEM(whole, bf16),
            pltpu.VMEM((4, tiles, rows_x + 2 * HALO, LANES), bf16),
            index_scratch,
        ],
        15 * 10**9,
    )

    def fetch(at):
        own, same, core, cross = (pieces[i * len(sizes) + at] for i in range(4))
        return [own, send(same, to_same), send(core, to_core), send(cross, to_cross)]

    def correlate(fields, received, begin, end, offset, last, buffer):
        count = end - begin
        operands = [pinned(x) for x in fields + received]
        in_specs = [VMEM_SPEC] * len(operands)
        aliases = {}
        if last:
            out_shape = jax.ShapeDtypeStruct((1, lags, width, rows_y), f32)
            out_spec = pl.BlockSpec(
                (1, lags, width, count * LANES), lambda i: (0, 0, 0, begin // count)
            )
            if buffer is not None:
                in_specs.append(pl.BlockSpec(memory_space=pl.ANY))
                aliases = {len(operands): 0}
                operands.append(buffer)
        else:
            out_shape = pltpu.VMEM((lags, count, width, LANES), bf16)
            out_spec = VMEM_SPEC
        return pl.pallas_call(
            functools.partial(
                correlate_kernel,
                width=width,
                begin=offset,
                tiles=count,
                partial=bool(received),
                scale=factor if last else None,
            ),
            out_shape=out_shape,
            grid=(1,),
            in_specs=in_specs,
            out_specs=out_spec,
            scratch_shapes=[pltpu.VMEM((16, height, LANES), f32)],
            input_output_aliases=aliases,
            compiler_params=pltpu.CompilerParams(vmem_limit_bytes=8 * 2**20),
            cost_estimate=pl.CostEstimate(flops=10**9, bytes_accessed=10**6, transcendentals=0),
            name="correlate",
        )(*operands)

    image = None
    received = [[]] * len(groups)
    for step in range(strips):
        last = step == strips - 1
        fields = {}
        for g, (begin, end) in enumerate(groups):
            if step == 0:
                at, offset = g, 0
            else:
                n = [n for n, cut in enumerate(later) if cut[0] <= begin < cut[1]][0]
                at, offset = len(groups) + (step - 1) * len(later) + n, begin - later[n][0]
            if at not in fields:
                fields[at] = fetch(at)
            parts = fields[at]
            result = correlate(parts, received[g], begin, end, offset, last, image)
            if last:
                image = result
            else:
                received[g] = [send(result, onward)]
    return image


def solution(mesh):
    return jax.shard_map(
        shards,
        mesh=mesh,
        in_specs=(
            P(None, "freq", None, None, None),
            P(None, "freq", None, None, None),
            P("depth", None, None),
            P(),
            P(),
        ),
        out_specs=P("depth", None, "freq", None),
        check_vma=False,
    )
```

```python
import functools
import math

import jax
import jax.numpy as jnp
import ml_dtypes
import numpy as np
from jax import lax
from jax.experimental import pallas as pl
from jax.experimental.pallas import tpu as pltpu
from jax.sharding import PartitionSpec as P

LAG = 7
HALO = 8
LANES = 128
AXES = ("depth", "freq")
VMEM_BYTES = 24 * 2**20


RADIX = 4
BLOCKS_X = 2
BLOCKS_Y = 2


def residues(length):
    found = [np.arange(residue, length, RADIX) for residue in range(RADIX)]
    found[3] = found[3][::-1]
    return found


def residue_tables(length):
    position = np.arange(length, dtype=np.int64)
    product = position[:, None] * position[None, :] % length
    angles = product.astype(np.float32) * np.float32(2.0 * math.pi / length)
    factor = np.float32(1.0 / math.sqrt(length))
    cos, sin = np.cos(angles) * factor, np.sin(angles) * factor
    tables = []
    for residue in residues(length):
        c, s = (t[residue, : length // RADIX] for t in (cos, sin))
        tables.append(np.block([[c, s], [-s, c]]).astype(ml_dtypes.bfloat16))
    return np.stack(tables)


def wavenumbers_squared(length):
    position = np.arange(length)
    signed = np.where(position < length // 2, position, position - length)
    wave = signed.astype(np.float32) * np.float32(2.0 * math.pi / length)
    squared = wave * wave
    return np.concatenate([squared[residue] for residue in residues(length)[:3]])


def mix_forward(re, im):
    sum_re, dif_re = re[0] + re[2], re[0] - re[2]
    sum_im, dif_im = im[0] + im[2], im[0] - im[2]
    odd_re, gap_re = re[1] + re[3], re[1] - re[3]
    odd_im, gap_im = im[1] + im[3], im[1] - im[3]
    return (
        (sum_re + odd_re, sum_im + odd_im),
        (dif_re + gap_im, dif_im - gap_re),
        (sum_re - odd_re, sum_im - odd_im),
        (dif_re - gap_im, dif_im + gap_re),
    )


def mix_inverse(re, im):
    found = mix_forward(re, im)
    return found[0], found[3], found[2], found[1]


Q_MAX = 14.0


def fit(function, degree):
    cheb = np.polynomial.chebyshev.Chebyshev.interpolate(
        lambda t: function((t + 1.0) * Q_MAX / 2), degree
    )
    return [float(v) for v in np.polynomial.chebyshev.cheb2poly(cheb.coef)]


COS_FIT = fit(lambda q: np.cos(np.sqrt(q)), 7)
SINC_FIT = fit(lambda q: np.sinc(np.sqrt(q) / np.pi), 7)


def horner(coefficients, t):
    total = jnp.full_like(t, coefficients[-1])
    for value in coefficients[-2::-1]:
        total = total * t + value
    return total


def cos_sin(square, root):
    t = square * (2.0 / Q_MAX) - 1.0
    return horner(COS_FIT, t), horner(SINC_FIT, t) * root


def lookup(table_row, codes):
    rows = codes.shape[0]
    parts = []
    for tile in range(codes.shape[1] // LANES):
        index = codes[:, tile * LANES : (tile + 1) * LANES]
        source = jnp.broadcast_to(table_row, (rows, LANES))
        parts.append(jnp.take_along_axis(source, index, axis=1, mode="promise_in_bounds"))
    return parts


def turned(kind, a, b, cos, sin):
    if kind == 0:
        return a * cos - b * sin, a * sin + b * cos
    return a * cos + b * sin, b * cos - a * sin


def extent(ref):
    rows_x, rows_y = ref.shape[1], ref.shape[2]
    return rows_x // RADIX, rows_y // RADIX, rows_y // BLOCKS_Y


def forward_x(field, mid, left_x):
    part_x, _, block_y = extent(field)
    for i in range(BLOCKS_Y):
        cols = slice(i * block_y, (i + 1) * block_y)
        for kind in range(2):
            re, im = (
                [field[2 * kind + j, q * part_x : (q + 1) * part_x, cols] for q in range(RADIX)]
                for j in range(2)
            )
            for r, mixed in enumerate(mix_forward(re, im)):
                mixed = jnp.concatenate(mixed, axis=0)
                out = jnp.dot(left_x[r], mixed, preferred_element_type=jnp.float32)
                mid[2 * kind : 2 * kind + 2, r * part_x : (r + 1) * part_x, cols] = out.astype(
                    jnp.bfloat16
                ).reshape(2, part_x, block_y)


def fill_phases(angular, base, wave_x, wave_y, phases):
    reach = angular * base
    reach = reach * reach
    part = wave_x.shape[0] // 3

    def block(i, carry):
        rows = pl.ds(pl.multiple_of(i * part, part), part)
        q = reach - wave_x[rows, :] - wave_y[0:1, :]
        root = jnp.sqrt(jnp.abs(q))
        cos, sin = cos_sin(q, root)
        phases[0, rows] = jnp.where(q > 0.0, cos, jnp.exp(-root))
        phases[1, rows] = jnp.where(q > 0.0, sin, 0.0)
        return carry

    lax.fori_loop(0, 3, block, 0)


def along_y(mid, phases, left_y, right_y):
    part_x, part_y, _ = extent(mid)
    lanes = [slice(q * part_y, (q + 1) * part_y) for q in range(RADIX)]
    for i in range(RADIX):
        rows = slice(i * part_x, (i + 1) * part_x)
        same = slice(part_x, 2 * part_x) if i == 3 else rows
        re, im = (
            [jnp.concatenate([mid[j, rows, at], mid[2 + j, rows, at]], axis=0) for at in lanes]
            for j in range(2)
        )
        back = []
        for r, mixed in enumerate(mix_forward(re, im)):
            mixed = jnp.concatenate(mixed, axis=1)
            spectrum = jnp.dot(mixed, right_y[r], preferred_element_type=jnp.float32)
            at = lanes[1 if r == 3 else r]
            phase_re, phase_im = phases[0, same, at], phases[1, same, at]
            pieces = []
            for kind in range(2):
                part = spectrum[kind * part_x : (kind + 1) * part_x]
                new = turned(kind, part[:, :part_y], part[:, part_y:], phase_re, phase_im)
                pieces.append(jnp.concatenate(new, axis=1).astype(jnp.bfloat16))
            shifted = jnp.concatenate(pieces, axis=0)
            back.append(jnp.dot(shifted, left_y[r], preferred_element_type=jnp.float32))
        back_re = [value[:, :part_y] for value in back]
        back_im = [value[:, part_y:] for value in back]
        for at, mixed in zip(lanes, mix_inverse(back_re, back_im)):
            for j in range(2):
                value = mixed[j].astype(jnp.bfloat16)
                for kind in range(2):
                    mid[2 * kind + j, rows, at] = value[kind * part_x : (kind + 1) * part_x]


def inverse_x(mid, right_x, sink):
    part_x, _, block_y = extent(mid)
    for i in range(BLOCKS_Y):
        cols = slice(i * block_y, (i + 1) * block_y)
        for kind in range(2):
            back = [
                jnp.dot(
                    right_x[r],
                    mid[2 * kind : 2 * kind + 2, r * part_x : (r + 1) * part_x, cols].reshape(
                        2 * part_x, block_y
                    ),
                    preferred_element_type=jnp.float32,
                )
                for r in range(RADIX)
            ]
            back_re = [value[:part_x] for value in back]
            back_im = [value[part_x:] for value in back]
            sink(i, cols, kind, mix_inverse(back_re, back_im))


def screen_tables(angular, base, levels):
    angle = angular * (levels[0:1, :] - base)
    return cos_sin(angle * angle, angle)


def fill_index(index, pair, flag):
    for value, source in ((flag, pair[0]), (jnp.logical_not(flag), pair[1])):

        @pl.when(value)
        def _(source=source):
            index[...] = source[...].astype(jnp.float32).astype(jnp.int32)


def screens_of(tables, index, rows, cols):
    return [jnp.concatenate(lookup(table, index[rows, cols]), axis=1) for table in tables]


def put_screened(tables, index, field, padded=None):
    part_x, _, block_y = extent(field)
    kept = {}

    def sink(i, cols, kind, parts):
        if i not in kept:
            kept.clear()
            kept[i] = [
                screens_of(tables, index, slice(p * part_x, (p + 1) * part_x), cols)
                for p in range(RADIX)
            ]
        done = [turned(kind, a, b, *kept[i][p]) for p, (a, b) in enumerate(parts)]
        for j in range(2):
            for p in range(RADIX):
                at = slice(p * part_x, (p + 1) * part_x)
                field[2 * kind + j, at, cols] = done[p][j].astype(jnp.bfloat16)
            if padded is not None:
                edge = jnp.zeros((HALO, block_y), jnp.float32)
                whole = jnp.concatenate([edge, *(d[j] for d in done), edge], axis=0)
                whole = whole.astype(jnp.bfloat16)
                for k in range(block_y // LANES):
                    padded[2 * kind + j, i * (block_y // LANES) + k] = whole[
                        :, k * LANES : (k + 1) * LANES
                    ]

    return sink


def prepare_kernel(place, angular_ref, source, receiver, mine, from_core, levels, *refs, shots):
    count = (len(refs) - 7) // 2
    tables, refs = refs[:count], refs[count:]
    wave_x, wave_y, top, mid, means, phases = refs[:6]
    kept, index = refs[6:-1], refs[-1]
    angular, my_core = angular_ref[0], place[1]
    for table, copy in zip(tables, kept):
        copy[...] = table[...]
    top[0:2] = source[0, 0]
    top[2:4] = receiver[0, 0]
    rows_x, rows_y = index.shape
    for p in range(shots):
        fill_index(index, (mine, from_core), my_core == p)
        if p == 0:
            forward_x(top, mid, tables[0])
        value = functools.reduce(jnp.add, lookup(levels[0:1, :], index[...]))
        base = jnp.sum(jnp.sum(value.reshape(rows_x // 8, 8, LANES), axis=0)) / (rows_x * rows_y)
        means[p : p + 1, :] = jnp.full((1, LANES), base, jnp.float32)
        fill_phases(angular, base, wave_x, wave_y, phases.at[p])


def lead_kernel(
    place, angular_ref, first, far_a, far_b, means, levels, left_x, right_x, left_y, right_y,
    wave_x, wave_y, before, mid, field, index, phases,
):
    angular, my_core = angular_ref[0], place[1]

    def put_plain(i, cols, kind, parts):
        part_x = extent(field)[0]
        for p, values in enumerate(parts):
            for j in range(2):
                before[2 * kind + j, p * part_x : (p + 1) * part_x, cols] = values[j]

    @pl.when(place[0] > 0)
    def _():
        fill_phases(angular, means[0:1, 0:1], wave_x, wave_y, phases)
        mid[...] = first[...]
        along_y(mid, phases, left_y, right_y)
        fill_index(index, (far_a, far_b), my_core == 0)
        tables = screen_tables(angular, means[0:1, 0:1], levels)
        inverse_x(mid, right_x, put_screened(tables, index, field))
        forward_x(field, mid, left_x)
        fill_phases(angular, means[1:2, 0:1], wave_x, wave_y, phases)
        along_y(mid, phases, left_y, right_y)
        inverse_x(mid, right_x, put_plain)


def planes_kernel(place, angular_ref, *refs, shots, strips, width, groups, later):
    refs = list(refs)
    top, before, far_a, far_b, far_means, near_a, near_b, means, phases, levels = refs[:10]
    left_x, right_x, left_y, right_y = refs[10:14]
    outs = refs[14:-4]
    field, mid, padded, index = refs[-4:]
    angular, my_core, parity, spot = angular_ref[0], place[1], place[2], place[3]

    @pl.when(place[0] == 0)
    def _():
        field[...] = top[...]

    @pl.when(place[0] > 0)
    def _():
        fill_index(index, (far_a, far_b), my_core == 1)
        tables = screen_tables(angular, far_means[1:2, 0:1], levels)
        block = 128

        def part(i, carry):
            rows = pl.ds(pl.multiple_of(i * block, block), block)
            cos, sin = screens_of(tables, index, rows, slice(None))
            for kind in range(2):
                new = turned(kind, before[2 * kind, rows], before[2 * kind + 1, rows], cos, sin)
                for j in range(2):
                    field[2 * kind + j, rows] = new[j].astype(jnp.bfloat16)
            return carry

        lax.fori_loop(0, index.shape[0] // block, part, 0)

    def emit(target, to):
        for s in range(strips):
            p = lax.rem(spot + (strips - 1 - s), strips)
            strip = jnp.where(p == 0, 0, jnp.where(p <= strips // 2, 2 * p - 1, 2 * (strips - p)))
            start = pl.multiple_of((2 * strip + to) * width, 16)
            for n, (first, last) in enumerate(groups if s == 0 else later):
                at = n if s == 0 else len(groups) + (s - 1) * len(later) + n
                out = outs[target * (len(groups) + (strips - 1) * len(later)) + at]
                for tile in range(first, last):
                    for part in range(4):
                        out[part, tile - first] = padded[part, tile, pl.ds(start, width + 2 * HALO)]

    for plane in range(shots):
        forward_x(field, mid, left_x)
        fill_index(index, (near_a, near_b), my_core == plane)
        along_y(mid, phases.at[plane], left_y, right_y)
        tables = screen_tables(angular, means[plane : plane + 1, 0:1], levels)
        inverse_x(mid, right_x, put_screened(tables, index, field, padded))

        @pl.when(my_core == plane)
        def _():
            emit(0, parity)
            emit(1, 1 - parity)

        @pl.when(my_core != plane)
        def _():
            emit(2, parity)
            emit(3, 1 - parity)


def correlate_kernel(*refs, width, begin, tiles, partial, scale):
    fields, out, wide = refs[:4], refs[-2], refs[-1]
    for tile in range(tiles):
        lanes = slice(tile * LANES, (tile + 1) * LANES)
        for m in range(4):
            for part in range(4):
                wide[m * 4 + part] = fields[m][part, begin + tile].astype(jnp.float32)
        for lag in range(2 * LAG + 1):
            shift = lag - LAG
            total = None
            for m in range(4):
                for part in range(2):
                    term = (
                        wide[m * 4 + part, HALO - shift : HALO - shift + width]
                        * wide[m * 4 + 2 + part, HALO + shift : HALO + shift + width]
                    )
                    total = term if total is None else total + term
            if partial:
                total = total + refs[4][lag, tile].astype(jnp.float32)
            if scale is not None:
                out[0, lag, :, lanes] = total * scale
            else:
                out[lag, tile] = total.astype(out.dtype)


def window_kernel(place, anchors, codes, mine, other, held, arrived, *, blocks):
    rows_x, rows_y = mine.shape
    rows = rows_x // blocks
    copies = []
    for i in range(blocks):
        for flip in range(2):
            shot = jnp.abs(place[1] - flip)
            at_x = pl.multiple_of(anchors[shot, 0] // rows_x * rows_x, rows_x) + i * rows
            at_y = pl.multiple_of(anchors[shot, 1] // rows_y * rows_y, rows_y)
            copy = pltpu.make_async_copy(
                codes.at[0, pl.ds(at_x, rows), pl.ds(at_y, rows_y)],
                held.at[flip, pl.ds(i * rows, rows)],
                arrived.at[flip, i],
            )
            copy.start()
            copies.append(copy)
    for i in range(blocks):
        for flip, out in enumerate((mine, other)):
            copies[2 * i + flip].wait()
            at = slice(i * rows, (i + 1) * rows)
            out[at] = held[flip, at].astype(jnp.float32).astype(out.dtype)


def pinned(x):
    return pltpu.with_memory_space_constraint(x, pltpu.VMEM)


def unpinned(x):
    return pltpu.with_memory_space_constraint(x, pltpu.HBM)


VMEM_SPEC = pl.BlockSpec(memory_space=pltpu.VMEM)


def call(kernel, name, scalars, operands, outs, scratch, flops):
    return pl.pallas_call(
        kernel,
        out_shape=[pltpu.VMEM(shape, dtype) for shape, dtype in outs],
        grid_spec=pltpu.PrefetchScalarGridSpec(
            num_scalar_prefetch=len(scalars),
            grid=(1,),
            in_specs=[VMEM_SPEC] * len(operands),
            out_specs=[VMEM_SPEC] * len(outs),
            scratch_shapes=scratch,
        ),
        compiler_params=pltpu.CompilerParams(vmem_limit_bytes=VMEM_BYTES),
        cost_estimate=pl.CostEstimate(flops=flops, bytes_accessed=10**6, transcendentals=0),
        name=name,
    )(*scalars, *(pinned(x) for x in operands))


def windows(place, anchors, slowness_codes, rows_x, rows_y):
    blocks = 4
    return pl.pallas_call(
        functools.partial(window_kernel, blocks=blocks),
        out_shape=[
            pltpu.VMEM((rows_x, rows_y), jnp.bfloat16),
            pltpu.HBM((rows_x, rows_y), jnp.bfloat16),
        ],
        grid_spec=pltpu.PrefetchScalarGridSpec(
            num_scalar_prefetch=2,
            grid=(1,),
            in_specs=[pl.BlockSpec(memory_space=pl.ANY)],
            out_specs=[VMEM_SPEC, VMEM_SPEC],
            scratch_shapes=[
                pltpu.VMEM((2, rows_x, rows_y), jnp.int32),
                pltpu.SemaphoreType.DMA((2, blocks)),
            ],
        ),
        compiler_params=pltpu.CompilerParams(vmem_limit_bytes=VMEM_BYTES),
        name="windows",
    )(place, anchors, unpinned(slowness_codes))


def shards(source_top, receiver_top, slowness_codes, slowness_table, anchors):
    shots, _, _, rows_x, rows_y = source_top.shape
    freq_count = lax.axis_size("freq")
    depth_count = lax.axis_size("depth")
    strips = freq_count // 2
    width = rows_x // freq_count
    height = width + 2 * HALO
    lags = 2 * LAG + 1
    tiles = rows_y // LANES
    groups = [(0, tiles // 2), (tiles // 2, tiles)]
    later = groups
    factor = 1.0 / math.sqrt(2.0 * shots * freq_count)
    depth_index = lax.axis_index("depth")
    freq_index = lax.axis_index("freq")
    my_core = depth_index % shots
    group = depth_index // shots
    bf16, f32 = jnp.bfloat16, jnp.float32

    def number(group_at, core_at, strip_at, parity_at):
        return (group_at * shots + core_at) * freq_count + strip_at * 2 + parity_at

    def pairs(move, core):
        found = []
        for g in range(depth_count // shots):
            for c in range(shots):
                for z in range(strips):
                    for x in range(2):
                        to = move(g, c, z, x)
                        if core in (None, c) and to is not None:
                            found.append((number(g, c, z, x), number(*to)))
        return found

    def send(value, move, core=None):
        return lax.ppermute(value, AXES, pairs(move, core))

    def to_core(g, c, z, x):
        return (g, 1 - c, z, x)

    def to_same(g, c, z, x):
        return (g, c, z, 1 - x)

    def to_cross(g, c, z, x):
        return (g, 1 - c, z, 1 - x)

    def up(g, c, z, x):
        return (1, c, z, x) if g == 0 else None

    ring = [0] + list(range(1, strips, 2)) + list(range(2, strips, 2))[::-1]
    spots = {z: p for p, z in enumerate(ring)}

    def onward(g, c, z, x):
        return (g, c, ring[(spots[z] + 1) % strips], x)

    my_strip = freq_index // 2
    spot = jnp.where(
        my_strip == 0,
        0,
        jnp.where(my_strip % 2 == 1, (my_strip + 1) // 2, strips - my_strip // 2),
    )
    place = jnp.stack([group, my_core, freq_index % 2, spot]).astype(jnp.int32)
    angular = (math.pi * (0.45 + 0.5 * (freq_index.astype(f32) + 0.5) / freq_count))[None]
    scalars = (place, angular)

    mine, other = windows(place, anchors, slowness_codes, rows_x, rows_y)
    from_core = send(other, to_core)
    near = (mine, from_core)
    far_first = (send(mine, up, 0), send(from_core, up, 1))

    levels = jnp.pad(slowness_table, (0, LANES - slowness_table.shape[0]))[None]
    tables = []
    for length in (rows_x,) if rows_x == rows_y else (rows_x, rows_y):
        left = residue_tables(length)
        tables += [jnp.asarray(left), jnp.asarray(np.swapaxes(left, 1, 2))]
    wave_x = jnp.asarray(wavenumbers_squared(rows_x)[:, None])
    wave_y = jnp.asarray(wavenumbers_squared(rows_y)[None])
    whole = (4, rows_x, rows_y)
    phase_shape = (2, wave_x.shape[0], wave_y.shape[1])
    index_scratch = pltpu.VMEM((rows_x, rows_y), jnp.int32)
    top_spec = pl.BlockSpec(
        (1, 1, 2, rows_x, rows_y), lambda i, place, angular: (place[1], 0, 0, 0, 0)
    )
    prepared = pl.pallas_call(
        functools.partial(prepare_kernel, shots=shots),
        out_shape=[
            pltpu.VMEM(whole, bf16),
            pltpu.VMEM(whole, bf16),
            pltpu.VMEM((8, LANES), f32),
            pltpu.VMEM((shots, *phase_shape), f32),
            *(pltpu.VMEM(t.shape, t.dtype) for t in tables),
        ],
        grid_spec=pltpu.PrefetchScalarGridSpec(
            num_scalar_prefetch=2,
            grid=(1,),
            in_specs=[top_spec] * 2 + [VMEM_SPEC] * (5 + len(tables)),
            out_specs=[VMEM_SPEC] * (4 + len(tables)),
            scratch_shapes=[index_scratch],
        ),
        compiler_params=pltpu.CompilerParams(vmem_limit_bytes=VMEM_BYTES),
        cost_estimate=pl.CostEstimate(flops=4 * 10**9, bytes_accessed=10**6, transcendentals=0),
        name="prepare",
    )(
        *scalars, unpinned(source_top), unpinned(receiver_top), pinned(mine), pinned(from_core),
        levels, *(unpinned(t) for t in tables), wave_x, wave_y,
    )
    top, first, means, phases, *tables = prepared
    tables = list(tables) if len(tables) == 4 else list(tables) * 2

    far_means = send(means, up)
    mine_later, from_core_later, _ = lax.optimization_barrier((mine, from_core, means))
    far_second = (send(mine_later, up, 1), send(from_core_later, up, 0))

    (before,) = call(
        lead_kernel,
        "lead",
        scalars,
        [first, *far_first, far_means, levels, *tables, wave_x, wave_y],
        [(whole, f32)],
        [pltpu.VMEM(whole, bf16), pltpu.VMEM(whole, bf16), index_scratch, pltpu.VMEM(phase_shape, f32)],
        15 * 10**9,
    )
    sizes = [end - begin for begin, end in groups]
    sizes += [end - begin for begin, end in later] * (strips - 1)
    pieces = call(
        functools.partial(
            planes_kernel, shots=shots, strips=strips, width=width, groups=groups, later=later
        ),
        "planes",
        scalars,
        [top, before, *far_second, far_means, *near, means, phases, levels, *tables],
        [((4, size, height, LANES), bf16) for _ in range(4) for size in sizes],
        [
            pltpu.VMEM(whole, bf16),
            pltpu.VMEM(whole, bf16),
            pltpu.VMEM((4, tiles, rows_x + 2 * HALO, LANES), bf16),
            index_scratch,
        ],
        15 * 10**9,
    )

    def fetch(at):
        own, same, core, cross = (pieces[i * len(sizes) + at] for i in range(4))
        return [own, send(same, to_same), send(core, to_core), send(cross, to_cross)]

    def correlate(fields, received, begin, end, offset, last, buffer, before):
        count = end - begin
        operands = [pinned(x) for x in fields + received]
        in_specs = [VMEM_SPEC] * len(operands)
        if before is not None and False:
            operands.append(pinned(before))
            in_specs.append(VMEM_SPEC)
        aliases = {}
        if last:
            out_shape = jax.ShapeDtypeStruct((1, lags, width, rows_y), f32)
            out_spec = pl.BlockSpec(
                (1, lags, width, count * LANES), lambda i: (0, 0, 0, begin // count)
            )
            if buffer is not None:
                in_specs.append(pl.BlockSpec(memory_space=pl.ANY))
                aliases = {len(operands): 0}
                operands.append(buffer)
        else:
            out_shape = pltpu.VMEM((lags, count, width, LANES), bf16)
            out_spec = VMEM_SPEC
        return pl.pallas_call(
            functools.partial(
                correlate_kernel,
                width=width,
                begin=offset,
                tiles=count,
                partial=bool(received),
                scale=factor if last else None,
            ),
            out_shape=out_shape,
            grid=(1,),
            in_specs=in_specs,
            out_specs=out_spec,
            scratch_shapes=[pltpu.VMEM((16, height, LANES), f32)],
            input_output_aliases=aliases,
            compiler_params=pltpu.CompilerParams(vmem_limit_bytes=8 * 2**20),
            cost_estimate=pl.CostEstimate(flops=10**9, bytes_accessed=10**6, transcendentals=0),
            name="correlate",
        )(*operands)

    image = None
    before = None
    received = [[]] * len(groups)
    for step in range(strips):
        last = step == strips - 1
        fields = {}
        for g, (begin, end) in enumerate(groups):
            if step == 0:
                at, offset = g, 0
            else:
                n = [n for n, cut in enumerate(later) if cut[0] <= begin < cut[1]][0]
                at, offset = len(groups) + (step - 1) * len(later) + n, begin - later[n][0]
            if at not in fields:
                fields[at] = fetch(at)
            parts = fields[at]
            result = correlate(parts, received[g], begin, end, offset, last, image, before)
            if last:
                image = result
                before = None
            else:
                before = result
                received[g] = [send(result, onward)]
    return image


def solution(mesh):
    return jax.shard_map(
        shards,
        mesh=mesh,
        in_specs=(
            P(None, "freq", None, None, None),
            P(None, "freq", None, None, None),
            P("depth", None, None),
            P(),
            P(),
        ),
        out_specs=P("depth", None, "freq", None),
        check_vma=False,
    )
```

```python
import functools
import math

import jax
import jax.numpy as jnp
import ml_dtypes
import numpy as np
from jax import lax
from jax.experimental import pallas as pl
from jax.experimental.pallas import tpu as pltpu
from jax.sharding import PartitionSpec as P

LAG = 7
HALO = 8
LANES = 128
AXES = ("depth", "freq")
VMEM_BYTES = 24 * 2**20


RADIX = 4
BLOCKS_X = 2
BLOCKS_Y = 2


def residues(length):
    found = [np.arange(residue, length, RADIX) for residue in range(RADIX)]
    found[3] = found[3][::-1]
    return found


def residue_tables(length):
    position = np.arange(length, dtype=np.int64)
    product = position[:, None] * position[None, :] % length
    angles = product.astype(np.float32) * np.float32(2.0 * math.pi / length)
    factor = np.float32(1.0 / math.sqrt(length))
    cos, sin = np.cos(angles) * factor, np.sin(angles) * factor
    tables = []
    for residue in residues(length):
        c, s = (t[residue, : length // RADIX] for t in (cos, sin))
        tables.append(np.block([[c, s], [-s, c]]).astype(ml_dtypes.bfloat16))
    return np.stack(tables)


def wavenumbers_squared(length):
    position = np.arange(length)
    signed = np.where(position < length // 2, position, position - length)
    wave = signed.astype(np.float32) * np.float32(2.0 * math.pi / length)
    squared = wave * wave
    return np.concatenate([squared[residue] for residue in residues(length)[:3]])


def mix_forward(re, im):
    sum_re, dif_re = re[0] + re[2], re[0] - re[2]
    sum_im, dif_im = im[0] + im[2], im[0] - im[2]
    odd_re, gap_re = re[1] + re[3], re[1] - re[3]
    odd_im, gap_im = im[1] + im[3], im[1] - im[3]
    return (
        (sum_re + odd_re, sum_im + odd_im),
        (dif_re + gap_im, dif_im - gap_re),
        (sum_re - odd_re, sum_im - odd_im),
        (dif_re - gap_im, dif_im + gap_re),
    )


def mix_inverse(re, im):
    found = mix_forward(re, im)
    return found[0], found[3], found[2], found[1]


Q_MAX = 14.0


def fit(function, degree):
    cheb = np.polynomial.chebyshev.Chebyshev.interpolate(
        lambda t: function((t + 1.0) * Q_MAX / 2), degree
    )
    return [float(v) for v in np.polynomial.chebyshev.cheb2poly(cheb.coef)]


COS_FIT = fit(lambda q: np.cos(np.sqrt(q)), 7)
SINC_FIT = fit(lambda q: np.sinc(np.sqrt(q) / np.pi), 7)


def horner(coefficients, t):
    total = jnp.full_like(t, coefficients[-1])
    for value in coefficients[-2::-1]:
        total = total * t + value
    return total


def cos_sin(square, root):
    t = square * (2.0 / Q_MAX) - 1.0
    return horner(COS_FIT, t), horner(SINC_FIT, t) * root


def lookup(table_row, codes):
    rows = codes.shape[0]
    parts = []
    for tile in range(codes.shape[1] // LANES):
        index = codes[:, tile * LANES : (tile + 1) * LANES]
        source = jnp.broadcast_to(table_row, (rows, LANES))
        parts.append(jnp.take_along_axis(source, index, axis=1, mode="promise_in_bounds"))
    return parts


def turned(kind, a, b, cos, sin):
    if kind == 0:
        return a * cos - b * sin, a * sin + b * cos
    return a * cos + b * sin, b * cos - a * sin


def extent(ref):
    rows_x, rows_y = ref.shape[1], ref.shape[2]
    return rows_x // RADIX, rows_y // RADIX, rows_y // BLOCKS_Y


def forward_x(load, mid, left_x):
    part_x, _, block_y = extent(mid)
    for i in range(BLOCKS_Y):
        cols = slice(i * block_y, (i + 1) * block_y)
        for kind in range(2):
            re, im = load(cols, kind)
            for r, mixed in enumerate(mix_forward(re, im)):
                mixed = jnp.concatenate(mixed, axis=0)
                out = jnp.dot(left_x[r], mixed, preferred_element_type=jnp.float32)
                mid[2 * kind : 2 * kind + 2, r * part_x : (r + 1) * part_x, cols] = out.astype(
                    jnp.bfloat16
                ).reshape(2, part_x, block_y)


def rows_of(ref):
    part_x = extent(ref)[0]
    return [slice(q * part_x, (q + 1) * part_x) for q in range(RADIX)]


def plainly(field):
    return lambda cols, kind: [[field[2 * kind + j, q, cols] for q in rows_of(field)] for j in range(2)]


def screening(before, tables, index):
    kept = {}

    def load(cols, kind):
        if cols.start not in kept:
            kept.clear()
            kept[cols.start] = [screens_of(tables, index, q, cols) for q in rows_of(before)]
        done = [
            turned(kind, before[2 * kind, q, cols], before[2 * kind + 1, q, cols], *screen)
            for q, screen in zip(rows_of(before), kept[cols.start])
        ]
        return [[value[j].astype(jnp.bfloat16) for value in done] for j in range(2)]

    return load


def fill_phases(angular, base, wave_x, wave_y, phases):
    reach = angular * base
    reach = reach * reach
    part = wave_x.shape[0] // 3

    def block(i, carry):
        rows = pl.ds(pl.multiple_of(i * part, part), part)
        q = reach - wave_x[rows, :] - wave_y[0:1, :]
        root = jnp.sqrt(jnp.abs(q))
        cos, sin = cos_sin(q, root)
        phases[0, rows] = jnp.where(q > 0.0, cos, jnp.exp(-root))
        phases[1, rows] = jnp.where(q > 0.0, sin, 0.0)
        return carry

    lax.fori_loop(0, 3, block, 0)


def along_y(mid, phases, left_y, right_y):
    part_x, part_y, _ = extent(mid)
    lanes = [slice(q * part_y, (q + 1) * part_y) for q in range(RADIX)]
    for i in range(RADIX):
        rows = slice(i * part_x, (i + 1) * part_x)
        same = slice(part_x, 2 * part_x) if i == 3 else rows
        re, im = (
            [jnp.concatenate([mid[j, rows, at], mid[2 + j, rows, at]], axis=0) for at in lanes]
            for j in range(2)
        )
        back = []
        for r, mixed in enumerate(mix_forward(re, im)):
            mixed = jnp.concatenate(mixed, axis=1)
            spectrum = jnp.dot(mixed, right_y[r], preferred_element_type=jnp.float32)
            at = lanes[1 if r == 3 else r]
            phase_re, phase_im = phases[0, same, at], phases[1, same, at]
            pieces = []
            for kind in range(2):
                part = spectrum[kind * part_x : (kind + 1) * part_x]
                new = turned(kind, part[:, :part_y], part[:, part_y:], phase_re, phase_im)
                pieces.append(jnp.concatenate(new, axis=1).astype(jnp.bfloat16))
            shifted = jnp.concatenate(pieces, axis=0)
            back.append(jnp.dot(shifted, left_y[r], preferred_element_type=jnp.float32))
        back_re = [value[:, :part_y] for value in back]
        back_im = [value[:, part_y:] for value in back]
        for at, mixed in zip(lanes, mix_inverse(back_re, back_im)):
            for j in range(2):
                value = mixed[j].astype(jnp.bfloat16)
                for kind in range(2):
                    mid[2 * kind + j, rows, at] = value[kind * part_x : (kind + 1) * part_x]


def inverse_x(mid, right_x, sink):
    part_x, _, block_y = extent(mid)
    for i in range(BLOCKS_Y):
        cols = slice(i * block_y, (i + 1) * block_y)
        for kind in range(2):
            back = [
                jnp.dot(
                    right_x[r],
                    mid[2 * kind : 2 * kind + 2, r * part_x : (r + 1) * part_x, cols].reshape(
                        2 * part_x, block_y
                    ),
                    preferred_element_type=jnp.float32,
                )
                for r in range(RADIX)
            ]
            back_re = [value[:part_x] for value in back]
            back_im = [value[part_x:] for value in back]
            sink(i, cols, kind, mix_inverse(back_re, back_im))


def screen_tables(angular, base, levels):
    angle = angular * (levels[0:1, :] - base)
    return cos_sin(angle * angle, angle)


def fill_index(index, pair, flag):
    for value, source in ((flag, pair[0]), (jnp.logical_not(flag), pair[1])):

        @pl.when(value)
        def _(source=source):
            index[...] = source[...].astype(jnp.float32).astype(jnp.int32)


def screens_of(tables, index, rows, cols):
    return [jnp.concatenate(lookup(table, index[rows, cols]), axis=1) for table in tables]


def put_screened(tables, index, field, padded=None):
    part_x, _, block_y = extent(field)
    kept = {}

    def sink(i, cols, kind, parts):
        if i not in kept:
            kept.clear()
            kept[i] = [
                screens_of(tables, index, slice(p * part_x, (p + 1) * part_x), cols)
                for p in range(RADIX)
            ]
        done = [turned(kind, a, b, *kept[i][p]) for p, (a, b) in enumerate(parts)]
        for j in range(2):
            for p in range(RADIX):
                at = slice(p * part_x, (p + 1) * part_x)
                field[2 * kind + j, at, cols] = done[p][j].astype(jnp.bfloat16)
            if padded is not None:
                edge = jnp.zeros((HALO, block_y), jnp.float32)
                whole = jnp.concatenate([edge, *(d[j] for d in done), edge], axis=0)
                whole = whole.astype(jnp.bfloat16)
                for k in range(block_y // LANES):
                    padded[2 * kind + j, i * (block_y // LANES) + k] = whole[
                        :, k * LANES : (k + 1) * LANES
                    ]

    return sink


def prepare_kernel(place, angular_ref, source, receiver, mine, from_core, levels, *refs, shots):
    count = (len(refs) - 7) // 2
    tables, refs = refs[:count], refs[count:]
    wave_x, wave_y, top, mid, means, phases = refs[:6]
    kept, index = refs[6:-1], refs[-1]
    angular, my_core = angular_ref[0], place[1]
    for table, copy in zip(tables, kept):
        copy[...] = table[...]
    top[0:2] = source[0, 0]
    top[2:4] = receiver[0, 0]
    rows_x, rows_y = index.shape
    for p in range(shots):
        fill_index(index, (mine, from_core), my_core == p)
        if p == 0:
            forward_x(plainly(top), mid, tables[0])
        value = functools.reduce(jnp.add, lookup(levels[0:1, :], index[...]))
        base = jnp.sum(jnp.sum(value.reshape(rows_x // 8, 8, LANES), axis=0)) / (rows_x * rows_y)
        means[p : p + 1, :] = jnp.full((1, LANES), base, jnp.float32)
        fill_phases(angular, base, wave_x, wave_y, phases.at[p])


def lead_kernel(
    place, angular_ref, first, far_a, far_b, means, levels, left_x, right_x, left_y, right_y,
    wave_x, wave_y, before, mid, field, index, phases,
):
    angular, my_core = angular_ref[0], place[1]

    def put_plain(i, cols, kind, parts):
        part_x = extent(field)[0]
        for p, values in enumerate(parts):
            for j in range(2):
                before[2 * kind + j, p * part_x : (p + 1) * part_x, cols] = values[j]

    @pl.when(place[0] > 0)
    def _():
        fill_phases(angular, means[0:1, 0:1], wave_x, wave_y, phases)
        mid[...] = first[...]
        along_y(mid, phases, left_y, right_y)
        fill_index(index, (far_a, far_b), my_core == 0)
        tables = screen_tables(angular, means[0:1, 0:1], levels)
        inverse_x(mid, right_x, put_screened(tables, index, field))
        forward_x(plainly(field), mid, left_x)
        fill_phases(angular, means[1:2, 0:1], wave_x, wave_y, phases)
        along_y(mid, phases, left_y, right_y)
        inverse_x(mid, right_x, put_plain)


def planes_kernel(place, angular_ref, *refs, shots, strips, width, groups):
    refs = list(refs)
    top, before, far_a, far_b, far_means, near_a, near_b, means, phases, levels = refs[:10]
    left_x, right_x, left_y, right_y = refs[10:14]
    padded_planes, outs = refs[14 : 14 + shots], refs[14 + shots : -3]
    field, mid, index = refs[-3:]
    angular, my_core, parity, spot = angular_ref[0], place[1], place[2], place[3]

    @pl.when(place[0] == 0)
    def _():
        forward_x(plainly(top), mid, left_x)

    @pl.when(place[0] > 0)
    def _():
        fill_index(index, (far_a, far_b), my_core == 1)
        tables = screen_tables(angular, far_means[1:2, 0:1], levels)
        forward_x(screening(before, tables, index), mid, left_x)

    for plane in range(shots):
        if plane > 0:
            forward_x(plainly(field), mid, left_x)
        fill_index(index, (near_a, near_b), my_core == plane)
        along_y(mid, phases.at[plane], left_y, right_y)
        tables = screen_tables(angular, means[plane : plane + 1, 0:1], levels)
        inverse_x(mid, right_x, put_screened(tables, index, field, padded_planes[plane]))
    hand_out(place, padded_planes, outs, 0, 1, strips, width, groups)


def strip_start(spot, step, strips, width, parity):
    p = lax.rem(spot + (strips - 1 - step), strips)
    strip = jnp.where(p == 0, 0, jnp.where(p <= strips // 2, 2 * p - 1, 2 * (strips - p)))
    return pl.multiple_of((2 * strip + parity) * width, 16)


def hand_out(place, padded_planes, outs, begin, end, strips, width, groups):
    my_core, parity, spot = place[1], place[2], place[3]
    for core in range(2):

        @pl.when(my_core == core)
        def _(core=core):
            for target in range(4):
                padded = padded_planes[core if target < 2 else 1 - core]
                to = parity if target % 2 == 0 else 1 - parity
                for step in range(begin, end):
                    start = strip_start(spot, step, strips, width, to)
                    for g, (first, last) in enumerate(groups):
                        out = outs[(target * (end - begin) + step - begin) * len(groups) + g]
                        for tile in range(first, last):
                            for part in range(4):
                                out[part, tile - first] = padded[
                                    part, tile, pl.ds(start, width + 2 * HALO)
                                ]


def strips_kernel(place, *refs, shots, strips, width, groups):
    hand_out(place, refs[:shots], refs[shots:], 1, strips, strips, width, groups)


def correlate_kernel(*refs, width, tiles, partial):
    fields, out, wide = refs[:4], refs[-2], refs[-1]
    for tile in range(tiles):
        for m in range(4):
            for part in range(4):
                wide[m * 4 + part] = fields[m][part, tile].astype(jnp.float32)
        for lag in range(2 * LAG + 1):
            shift = lag - LAG
            total = None
            for m in range(4):
                for part in range(2):
                    term = (
                        wide[m * 4 + part, HALO - shift : HALO - shift + width]
                        * wide[m * 4 + 2 + part, HALO + shift : HALO + shift + width]
                    )
                    total = term if total is None else total + term
            if partial:
                total = total + refs[4][lag, tile].astype(jnp.float32)
            out[lag, tile] = total.astype(out.dtype)


def finish_kernel(mine, received, *refs, scale):
    out = refs[-1]
    for tile in range(mine.shape[1]):
        lanes = slice(tile * LANES, (tile + 1) * LANES)
        for lag in range(mine.shape[0]):
            total = mine[lag, tile] + received[lag, tile].astype(jnp.float32)
            out[0, lag, :, lanes] = total * scale


def window_kernel(place, anchors, codes, mine, other, held, arrived, *, blocks):
    rows_x, rows_y = mine.shape
    rows = rows_x // blocks
    copies = []
    for i in range(blocks):
        for flip in range(2):
            shot = jnp.abs(place[1] - flip)
            at_x = pl.multiple_of(anchors[shot, 0] // rows_x * rows_x, rows_x) + i * rows
            at_y = pl.multiple_of(anchors[shot, 1] // rows_y * rows_y, rows_y)
            copy = pltpu.make_async_copy(
                codes.at[0, pl.ds(at_x, rows), pl.ds(at_y, rows_y)],
                held.at[flip, pl.ds(i * rows, rows)],
                arrived.at[flip, i],
            )
            copy.start()
            copies.append(copy)
    for i in range(blocks):
        for flip, out in enumerate((mine, other)):
            copies[2 * i + flip].wait()
            at = slice(i * rows, (i + 1) * rows)
            out[at] = held[flip, at].astype(jnp.float32).astype(out.dtype)


def pinned(x):
    return pltpu.with_memory_space_constraint(x, pltpu.VMEM)


def unpinned(x):
    return pltpu.with_memory_space_constraint(x, pltpu.HBM)


VMEM_SPEC = pl.BlockSpec(memory_space=pltpu.VMEM)


def call(kernel, name, scalars, operands, outs, scratch, flops):
    return pl.pallas_call(
        kernel,
        out_shape=[pltpu.VMEM(shape, dtype) for shape, dtype in outs],
        grid_spec=pltpu.PrefetchScalarGridSpec(
            num_scalar_prefetch=len(scalars),
            grid=(1,),
            in_specs=[VMEM_SPEC] * len(operands),
            out_specs=[VMEM_SPEC] * len(outs),
            scratch_shapes=scratch,
        ),
        compiler_params=pltpu.CompilerParams(vmem_limit_bytes=VMEM_BYTES),
        cost_estimate=pl.CostEstimate(flops=flops, bytes_accessed=10**6, transcendentals=0),
        name=name,
    )(*scalars, *(pinned(x) for x in operands))


def windows(place, anchors, slowness_codes, rows_x, rows_y):
    blocks = 4
    return pl.pallas_call(
        functools.partial(window_kernel, blocks=blocks),
        out_shape=[
            pltpu.VMEM((rows_x, rows_y), jnp.bfloat16),
            pltpu.HBM((rows_x, rows_y), jnp.bfloat16),
        ],
        grid_spec=pltpu.PrefetchScalarGridSpec(
            num_scalar_prefetch=2,
            grid=(1,),
            in_specs=[pl.BlockSpec(memory_space=pl.ANY)],
            out_specs=[VMEM_SPEC, VMEM_SPEC],
            scratch_shapes=[
                pltpu.VMEM((2, rows_x, rows_y), jnp.int32),
                pltpu.SemaphoreType.DMA((2, blocks)),
            ],
        ),
        compiler_params=pltpu.CompilerParams(vmem_limit_bytes=VMEM_BYTES),
        name="windows",
    )(place, anchors, unpinned(slowness_codes))


def shards(source_top, receiver_top, slowness_codes, slowness_table, anchors):
    shots, _, _, rows_x, rows_y = source_top.shape
    freq_count = lax.axis_size("freq")
    depth_count = lax.axis_size("depth")
    strips = freq_count // 2
    width = rows_x // freq_count
    height = width + 2 * HALO
    lags = 2 * LAG + 1
    tiles = rows_y // LANES
    groups = [(0, tiles // 2), (tiles // 2, tiles)]
    factor = 1.0 / math.sqrt(2.0 * shots * freq_count)
    depth_index = lax.axis_index("depth")
    freq_index = lax.axis_index("freq")
    my_core = depth_index % shots
    group = depth_index // shots
    bf16, f32 = jnp.bfloat16, jnp.float32

    def number(group_at, core_at, strip_at, parity_at):
        return (group_at * shots + core_at) * freq_count + strip_at * 2 + parity_at

    def pairs(move, core):
        found = []
        for g in range(depth_count // shots):
            for c in range(shots):
                for z in range(strips):
                    for x in range(2):
                        to = move(g, c, z, x)
                        if core in (None, c) and to is not None:
                            found.append((number(g, c, z, x), number(*to)))
        return found

    def send(value, move, core=None):
        return lax.ppermute(value, AXES, pairs(move, core))

    def to_core(g, c, z, x):
        return (g, 1 - c, z, x)

    def to_same(g, c, z, x):
        return (g, c, z, 1 - x)

    def to_cross(g, c, z, x):
        return (g, 1 - c, z, 1 - x)

    def up(g, c, z, x):
        return (1, c, z, x) if g == 0 else None

    ring = [0] + list(range(1, strips, 2)) + list(range(2, strips, 2))[::-1]
    spots = {z: p for p, z in enumerate(ring)}

    def onward(g, c, z, x):
        return (g, c, ring[(spots[z] + 1) % strips], x)

    my_strip = freq_index // 2
    spot = jnp.where(
        my_strip == 0,
        0,
        jnp.where(my_strip % 2 == 1, (my_strip + 1) // 2, strips - my_strip // 2),
    )
    place = jnp.stack([group, my_core, freq_index % 2, spot]).astype(jnp.int32)
    angular = (math.pi * (0.45 + 0.5 * (freq_index.astype(f32) + 0.5) / freq_count))[None]
    scalars = (place, angular)

    mine, other = windows(place, anchors, slowness_codes, rows_x, rows_y)
    from_core = send(other, to_core)
    near = (mine, from_core)
    far_first = (send(mine, up, 0), send(from_core, up, 1))

    levels = jnp.pad(slowness_table, (0, LANES - slowness_table.shape[0]))[None]
    tables = []
    for length in (rows_x,) if rows_x == rows_y else (rows_x, rows_y):
        left = residue_tables(length)
        tables += [jnp.asarray(left), jnp.asarray(np.swapaxes(left, 1, 2))]
    wave_x = jnp.asarray(wavenumbers_squared(rows_x)[:, None])
    wave_y = jnp.asarray(wavenumbers_squared(rows_y)[None])
    whole = (4, rows_x, rows_y)
    phase_shape = (2, wave_x.shape[0], wave_y.shape[1])
    index_scratch = pltpu.VMEM((rows_x, rows_y), jnp.int32)
    top_spec = pl.BlockSpec(
        (1, 1, 2, rows_x, rows_y), lambda i, place, angular: (place[1], 0, 0, 0, 0)
    )
    prepared = pl.pallas_call(
        functools.partial(prepare_kernel, shots=shots),
        out_shape=[
            pltpu.VMEM(whole, bf16),
            pltpu.VMEM(whole, bf16),
            pltpu.VMEM((8, LANES), f32),
            pltpu.VMEM((shots, *phase_shape), f32),
            *(pltpu.VMEM(t.shape, t.dtype) for t in tables),
        ],
        grid_spec=pltpu.PrefetchScalarGridSpec(
            num_scalar_prefetch=2,
            grid=(1,),
            in_specs=[top_spec] * 2 + [VMEM_SPEC] * (5 + len(tables)),
            out_specs=[VMEM_SPEC] * (4 + len(tables)),
            scratch_shapes=[index_scratch],
        ),
        compiler_params=pltpu.CompilerParams(vmem_limit_bytes=VMEM_BYTES),
        cost_estimate=pl.CostEstimate(flops=4 * 10**9, bytes_accessed=10**6, transcendentals=0),
        name="prepare",
    )(
        *scalars, unpinned(source_top), unpinned(receiver_top), pinned(mine), pinned(from_core),
        levels, *(unpinned(t) for t in tables), wave_x, wave_y,
    )
    top, first, means, phases, *tables = prepared
    tables = list(tables) if len(tables) == 4 else list(tables) * 2

    far_means = send(means, up)
    mine_later, from_core_later, _ = lax.optimization_barrier((mine, from_core, means))
    far_second = (send(mine_later, up, 1), send(from_core_later, up, 0))

    (before,) = call(
        lead_kernel,
        "lead",
        scalars,
        [first, *far_first, far_means, levels, *tables, wave_x, wave_y],
        [(whole, f32)],
        [pltpu.VMEM(whole, bf16), pltpu.VMEM(whole, bf16), index_scratch, pltpu.VMEM(phase_shape, f32)],
        15 * 10**9,
    )
    def strip_shapes(steps):
        return [
            ((4, end - begin, height, LANES), bf16)
            for _ in range(4 * steps)
            for begin, end in groups
        ]

    made = call(
        functools.partial(planes_kernel, shots=shots, strips=strips, width=width, groups=groups),
        "planes",
        scalars,
        [top, before, *far_second, far_means, *near, means, phases, levels, *tables],
        [((4, tiles, rows_x + 2 * HALO, LANES), bf16)] * shots + strip_shapes(1),
        [pltpu.VMEM(whole, bf16), pltpu.VMEM(whole, bf16), index_scratch],
        15 * 10**9,
    )
    padded_planes, first_strips = made[:shots], made[shots:]
    later_strips = call(
        functools.partial(strips_kernel, shots=shots, strips=strips, width=width, groups=groups),
        "strips",
        (place,),
        padded_planes,
        strip_shapes(strips - 1),
        [],
        10**9,
    )

    def fetch(step, g, after=None):
        if step == 0:
            own, same, core, cross = (first_strips[i * len(groups) + g] for i in range(4))
        else:
            own, same, core, cross = (
                later_strips[(i * (strips - 1) + step - 1) * len(groups) + g] for i in range(4)
            )
        if after is not None:
            own, same, core, cross, _ = lax.optimization_barrier((own, same, core, cross, after))
        return [own, send(same, to_same), send(core, to_core), send(cross, to_cross)]

    def correlate(fields, received, count, dtype):
        operands = fields + received
        return pl.pallas_call(
            functools.partial(
                correlate_kernel, width=width, tiles=count, partial=bool(received)
            ),
            out_shape=pltpu.VMEM((lags, count, width, LANES), dtype),
            grid=(1,),
            in_specs=[VMEM_SPEC] * len(operands),
            out_specs=VMEM_SPEC,
            scratch_shapes=[pltpu.VMEM((16, height, LANES), f32)],
            compiler_params=pltpu.CompilerParams(vmem_limit_bytes=8 * 2**20),
            cost_estimate=pl.CostEstimate(flops=10**9, bytes_accessed=10**6, transcendentals=0),
            name="correlate",
        )(*(pinned(x) for x in operands))

    def finish(own, received, begin, end, image):
        count = end - begin
        operands = [pinned(own), pinned(received)]
        in_specs = [VMEM_SPEC] * 2
        aliases = {}
        if image is not None:
            operands.append(image)
            in_specs.append(pl.BlockSpec(memory_space=pl.ANY))
            aliases = {2: 0}
        return pl.pallas_call(
            functools.partial(finish_kernel, scale=factor),
            out_shape=jax.ShapeDtypeStruct((1, lags, width, rows_y), f32),
            grid=(1,),
            in_specs=in_specs,
            out_specs=pl.BlockSpec(
                (1, lags, width, count * LANES), lambda i: (0, 0, 0, begin // count)
            ),
            input_output_aliases=aliases,
            compiler_params=pltpu.CompilerParams(vmem_limit_bytes=8 * 2**20),
            cost_estimate=pl.CostEstimate(flops=10**9, bytes_accessed=10**6, transcendentals=0),
            name="finish",
        )(*operands)

    image = None
    received = [[] for _ in groups]
    for step in range(strips - 1):
        for g, (begin, end) in enumerate(groups):
            result = correlate(fetch(step, g), received[g], end - begin, bf16)
            received[g] = [send(result, onward)]
    for g, (begin, end) in enumerate(groups):
        own = correlate(fetch(strips - 1, g, result), [], end - begin, f32)
        image = finish(own, received[g][0], begin, end, image)
    return image


def solution(mesh):
    return jax.shard_map(
        shards,
        mesh=mesh,
        in_specs=(
            P(None, "freq", None, None, None),
            P(None, "freq", None, None, None),
            P("depth", None, None),
            P(),
            P(),
        ),
        out_specs=P("depth", None, "freq", None),
        check_vma=False,
    )
```

```python
import functools
import math

import jax
import jax.numpy as jnp
import ml_dtypes
import numpy as np
from jax import lax
from jax.experimental import pallas as pl
from jax.experimental.pallas import tpu as pltpu
from jax.sharding import PartitionSpec as P

LAG = 7
HALO = 8
LANES = 128
AXES = ("depth", "freq")
VMEM_BYTES = 24 * 2**20


RADIX = 4
BLOCKS_X = 2
BLOCKS_Y = 2


def residues(length):
    found = [np.arange(residue, length, RADIX) for residue in range(RADIX)]
    found[3] = found[3][::-1]
    return found


def residue_tables(length):
    position = np.arange(length, dtype=np.int64)
    product = position[:, None] * position[None, :] % length
    angles = product.astype(np.float32) * np.float32(2.0 * math.pi / length)
    factor = np.float32(1.0 / math.sqrt(length))
    cos, sin = np.cos(angles) * factor, np.sin(angles) * factor
    tables = []
    for residue in residues(length):
        c, s = (t[residue, : length // RADIX] for t in (cos, sin))
        tables.append(np.block([[c, s], [-s, c]]).astype(ml_dtypes.bfloat16))
    return np.stack(tables)


def wavenumbers_squared(length):
    position = np.arange(length)
    signed = np.where(position < length // 2, position, position - length)
    wave = signed.astype(np.float32) * np.float32(2.0 * math.pi / length)
    squared = wave * wave
    return np.concatenate([squared[residue] for residue in residues(length)[:3]])


def mix_forward(re, im):
    sum_re, dif_re = re[0] + re[2], re[0] - re[2]
    sum_im, dif_im = im[0] + im[2], im[0] - im[2]
    odd_re, gap_re = re[1] + re[3], re[1] - re[3]
    odd_im, gap_im = im[1] + im[3], im[1] - im[3]
    return (
        (sum_re + odd_re, sum_im + odd_im),
        (dif_re + gap_im, dif_im - gap_re),
        (sum_re - odd_re, sum_im - odd_im),
        (dif_re - gap_im, dif_im + gap_re),
    )


def mix_inverse(re, im):
    found = mix_forward(re, im)
    return found[0], found[3], found[2], found[1]


Q_MAX = 14.0


def fit(function, degree):
    cheb = np.polynomial.chebyshev.Chebyshev.interpolate(
        lambda t: function((t + 1.0) * Q_MAX / 2), degree
    )
    return [float(v) for v in np.polynomial.chebyshev.cheb2poly(cheb.coef)]


COS_FIT = fit(lambda q: np.cos(np.sqrt(q)), 7)
SINC_FIT = fit(lambda q: np.sinc(np.sqrt(q) / np.pi), 7)


def horner(coefficients, t):
    total = jnp.full_like(t, coefficients[-1])
    for value in coefficients[-2::-1]:
        total = total * t + value
    return total


def cos_sin(square, root):
    t = square * (2.0 / Q_MAX) - 1.0
    return horner(COS_FIT, t), horner(SINC_FIT, t) * root


def lookup(table_row, codes):
    rows = codes.shape[0]
    parts = []
    for tile in range(codes.shape[1] // LANES):
        index = codes[:, tile * LANES : (tile + 1) * LANES]
        source = jnp.broadcast_to(table_row, (rows, LANES))
        parts.append(jnp.take_along_axis(source, index, axis=1, mode="promise_in_bounds"))
    return parts


def turned(kind, a, b, cos, sin):
    if kind == 0:
        return a * cos - b * sin, a * sin + b * cos
    return a * cos + b * sin, b * cos - a * sin


def extent(ref):
    rows_x, rows_y = ref.shape[1], ref.shape[2]
    return rows_x // RADIX, rows_y // RADIX, rows_y // BLOCKS_Y


def forward_x(load, mid, left_x):
    part_x, _, block_y = extent(mid)
    for i in range(BLOCKS_Y):
        cols = slice(i * block_y, (i + 1) * block_y)
        for kind in range(2):
            re, im = load(cols, kind)
            for r, mixed in enumerate(mix_forward(re, im)):
                mixed = jnp.concatenate(mixed, axis=0)
                out = jnp.dot(left_x[r], mixed, preferred_element_type=jnp.float32)
                mid[2 * kind : 2 * kind + 2, r * part_x : (r + 1) * part_x, cols] = out.astype(
                    jnp.bfloat16
                ).reshape(2, part_x, block_y)


def rows_of(ref):
    part_x = extent(ref)[0]
    return [slice(q * part_x, (q + 1) * part_x) for q in range(RADIX)]


def plainly(field):
    return lambda cols, kind: [[field[2 * kind + j, q, cols] for q in rows_of(field)] for j in range(2)]


def screening(before, tables, index):
    kept = {}

    def load(cols, kind):
        if cols.start not in kept:
            kept.clear()
            kept[cols.start] = [screens_of(tables, index, q, cols) for q in rows_of(before)]
        done = [
            turned(kind, before[2 * kind, q, cols], before[2 * kind + 1, q, cols], *screen)
            for q, screen in zip(rows_of(before), kept[cols.start])
        ]
        return [[value[j].astype(jnp.bfloat16) for value in done] for j in range(2)]

    return load


def fill_phases(angular, base, wave_x, wave_y, phases):
    reach = angular * base
    reach = reach * reach
    part = wave_x.shape[0] // 3

    def block(i, carry):
        rows = pl.ds(pl.multiple_of(i * part, part), part)
        q = reach - wave_x[rows, :] - wave_y[0:1, :]
        root = jnp.sqrt(jnp.abs(q))
        cos, sin = cos_sin(q, root)
        phases[0, rows] = jnp.where(q > 0.0, cos, jnp.exp(-root))
        phases[1, rows] = jnp.where(q > 0.0, sin, 0.0)
        return carry

    lax.fori_loop(0, 3, block, 0)


def along_y(mid, phases, left_y, right_y):
    part_x, part_y, _ = extent(mid)
    lanes = [slice(q * part_y, (q + 1) * part_y) for q in range(RADIX)]
    for i in range(RADIX):
        rows = slice(i * part_x, (i + 1) * part_x)
        same = slice(part_x, 2 * part_x) if i == 3 else rows
        re, im = (
            [jnp.concatenate([mid[j, rows, at], mid[2 + j, rows, at]], axis=0) for at in lanes]
            for j in range(2)
        )
        back = []
        for r, mixed in enumerate(mix_forward(re, im)):
            mixed = jnp.concatenate(mixed, axis=1)
            spectrum = jnp.dot(mixed, right_y[r], preferred_element_type=jnp.float32)
            at = lanes[1 if r == 3 else r]
            phase_re, phase_im = phases[0, same, at], phases[1, same, at]
            pieces = []
            for kind in range(2):
                part = spectrum[kind * part_x : (kind + 1) * part_x]
                new = turned(kind, part[:, :part_y], part[:, part_y:], phase_re, phase_im)
                pieces.append(jnp.concatenate(new, axis=1).astype(jnp.bfloat16))
            shifted = jnp.concatenate(pieces, axis=0)
            back.append(jnp.dot(shifted, left_y[r], preferred_element_type=jnp.float32))
        back_re = [value[:, :part_y] for value in back]
        back_im = [value[:, part_y:] for value in back]
        for at, mixed in zip(lanes, mix_inverse(back_re, back_im)):
            for j in range(2):
                value = mixed[j].astype(jnp.bfloat16)
                for kind in range(2):
                    mid[2 * kind + j, rows, at] = value[kind * part_x : (kind + 1) * part_x]


def inverse_x(mid, right_x, sink):
    part_x, _, block_y = extent(mid)
    for i in range(BLOCKS_Y):
        cols = slice(i * block_y, (i + 1) * block_y)
        for kind in range(2):
            back = [
                jnp.dot(
                    right_x[r],
                    mid[2 * kind : 2 * kind + 2, r * part_x : (r + 1) * part_x, cols].reshape(
                        2 * part_x, block_y
                    ),
                    preferred_element_type=jnp.float32,
                )
                for r in range(RADIX)
            ]
            back_re = [value[:part_x] for value in back]
            back_im = [value[part_x:] for value in back]
            sink(i, cols, kind, mix_inverse(back_re, back_im))


def screen_tables(angular, base, levels):
    angle = angular * (levels[0:1, :] - base)
    return cos_sin(angle * angle, angle)


def fill_index(index, pair, flag):
    for value, source in ((flag, pair[0]), (jnp.logical_not(flag), pair[1])):

        @pl.when(value)
        def _(source=source):
            index[...] = source[...].astype(jnp.float32).astype(jnp.int32)


def screens_of(tables, index, rows, cols):
    return [jnp.concatenate(lookup(table, index[rows, cols]), axis=1) for table in tables]


def put_screened(tables, index, field, padded=None):
    part_x, _, block_y = extent(field)
    kept = {}

    def sink(i, cols, kind, parts):
        if i not in kept:
            kept.clear()
            kept[i] = [
                screens_of(tables, index, slice(p * part_x, (p + 1) * part_x), cols)
                for p in range(RADIX)
            ]
        done = [turned(kind, a, b, *kept[i][p]) for p, (a, b) in enumerate(parts)]
        for j in range(2):
            for p in range(RADIX):
                at = slice(p * part_x, (p + 1) * part_x)
                field[2 * kind + j, at, cols] = done[p][j].astype(jnp.bfloat16)
            if padded is not None:
                edge = jnp.zeros((HALO, block_y), jnp.float32)
                whole = jnp.concatenate([edge, *(d[j] for d in done), edge], axis=0)
                whole = whole.astype(jnp.bfloat16)
                for k in range(block_y // LANES):
                    padded[2 * kind + j, i * (block_y // LANES) + k] = whole[
                        :, k * LANES : (k + 1) * LANES
                    ]

    return sink


def prepare_kernel(place, angular_ref, source, receiver, mine, from_core, levels, *refs, shots):
    count = (len(refs) - 7) // 2
    tables, refs = refs[:count], refs[count:]
    wave_x, wave_y, top, mid, means, phases = refs[:6]
    kept, index = refs[6:-1], refs[-1]
    angular, my_core = angular_ref[0], place[1]
    for table, copy in zip(tables, kept):
        copy[...] = table[...]
    top[0:2] = source[0, 0]
    top[2:4] = receiver[0, 0]
    rows_x, rows_y = index.shape[1:]
    for p in range(shots):
        fill_index(index.at[p], (mine, from_core), my_core == p)
        if p == 0:
            forward_x(plainly(top), mid, tables[0])
        value = functools.reduce(jnp.add, lookup(levels[0:1, :], index[p]))
        base = jnp.sum(jnp.sum(value.reshape(rows_x // 8, 8, LANES), axis=0)) / (rows_x * rows_y)
        means[p : p + 1, :] = jnp.full((1, LANES), base, jnp.float32)
        fill_phases(angular, base, wave_x, wave_y, phases.at[p])


def lead_kernel(
    place, angular_ref, first, far_a, far_b, means, levels, left_x, right_x, left_y, right_y,
    wave_x, wave_y, before, mid, field, index, phases,
):
    angular, my_core = angular_ref[0], place[1]

    def put_plain(i, cols, kind, parts):
        part_x = extent(field)[0]
        for p, values in enumerate(parts):
            for j in range(2):
                before[2 * kind + j, p * part_x : (p + 1) * part_x, cols] = values[j]

    @pl.when(place[0] > 0)
    def _():
        fill_phases(angular, means[0:1, 0:1], wave_x, wave_y, phases)
        mid[...] = first[...]
        along_y(mid, phases, left_y, right_y)
        fill_index(index, (far_a, far_b), my_core == 0)
        tables = screen_tables(angular, means[0:1, 0:1], levels)
        inverse_x(mid, right_x, put_screened(tables, index, field))
        forward_x(plainly(field), mid, left_x)
        fill_phases(angular, means[1:2, 0:1], wave_x, wave_y, phases)
        along_y(mid, phases, left_y, right_y)
        inverse_x(mid, right_x, put_plain)


def planes_kernel(place, angular_ref, *refs, shots, strips, width, groups):
    refs = list(refs)
    top, before, far_a, far_b, far_means, indices, means, phases, levels = refs[:9]
    left_x, right_x, left_y, right_y = refs[9:13]
    padded_planes, outs = refs[13 : 13 + shots], refs[13 + shots : -3]
    field, mid, index = refs[-3:]
    angular, my_core, parity, spot = angular_ref[0], place[1], place[2], place[3]

    @pl.when(place[0] == 0)
    def _():
        forward_x(plainly(top), mid, left_x)

    @pl.when(place[0] > 0)
    def _():
        fill_index(index, (far_a, far_b), my_core == 1)
        tables = screen_tables(angular, far_means[1:2, 0:1], levels)
        forward_x(screening(before, tables, index), mid, left_x)

    for plane in range(shots):
        if plane > 0:
            forward_x(plainly(field), mid, left_x)
        along_y(mid, phases.at[plane], left_y, right_y)
        tables = screen_tables(angular, means[plane : plane + 1, 0:1], levels)
        screened = put_screened(tables, indices.at[plane], field, padded_planes[plane])
        inverse_x(mid, right_x, screened)
    hand_out(place, padded_planes, outs, 0, 1, strips, width, groups)


def strip_start(spot, step, strips, width, parity):
    p = lax.rem(spot + (strips - 1 - step), strips)
    strip = jnp.where(p == 0, 0, jnp.where(p <= strips // 2, 2 * p - 1, 2 * (strips - p)))
    return pl.multiple_of((2 * strip + parity) * width, 16)


def hand_out(place, padded_planes, outs, begin, end, strips, width, groups):
    my_core, parity, spot = place[1], place[2], place[3]
    for core in range(2):

        @pl.when(my_core == core)
        def _(core=core):
            for target in range(4):
                padded = padded_planes[core if target < 2 else 1 - core]
                to = parity if target % 2 == 0 else 1 - parity
                for step in range(begin, end):
                    start = strip_start(spot, step, strips, width, to)
                    for g, (first, last) in enumerate(groups):
                        out = outs[(target * (end - begin) + step - begin) * len(groups) + g]
                        for tile in range(first, last):
                            for part in range(4):
                                out[part, tile - first] = padded[
                                    part, tile, pl.ds(start, width + 2 * HALO)
                                ]


def strips_kernel(place, *refs, shots, strips, width, groups):
    hand_out(place, refs[:shots], refs[shots:], 1, strips, strips, width, groups)


def correlate_kernel(*refs, width, tiles, partial):
    fields, out, wide = refs[:4], refs[-2], refs[-1]
    for tile in range(tiles):
        for m in range(4):
            for part in range(4):
                wide[m * 4 + part] = fields[m][part, tile].astype(jnp.float32)
        for lag in range(2 * LAG + 1):
            shift = lag - LAG
            total = None
            for m in range(4):
                for part in range(2):
                    term = (
                        wide[m * 4 + part, HALO - shift : HALO - shift + width]
                        * wide[m * 4 + 2 + part, HALO + shift : HALO + shift + width]
                    )
                    total = term if total is None else total + term
            if partial:
                total = total + refs[4][lag, tile].astype(jnp.float32)
            out[lag, tile] = total.astype(out.dtype)


def finish_kernel(mine, received, *refs, scale):
    out = refs[-1]
    for tile in range(mine.shape[1]):
        lanes = slice(tile * LANES, (tile + 1) * LANES)
        for lag in range(mine.shape[0]):
            total = mine[lag, tile] + received[lag, tile].astype(jnp.float32)
            out[0, lag, :, lanes] = total * scale


def window_kernel(place, anchors, codes, mine, other, held, arrived, *, blocks):
    rows_x, rows_y = mine.shape
    rows = rows_x // blocks
    copies = []
    for i in range(blocks):
        for flip in range(2):
            shot = jnp.abs(place[1] - flip)
            at_x = pl.multiple_of(anchors[shot, 0] // rows_x * rows_x, rows_x) + i * rows
            at_y = pl.multiple_of(anchors[shot, 1] // rows_y * rows_y, rows_y)
            copy = pltpu.make_async_copy(
                codes.at[0, pl.ds(at_x, rows), pl.ds(at_y, rows_y)],
                held.at[flip, pl.ds(i * rows, rows)],
                arrived.at[flip, i],
            )
            copy.start()
            copies.append(copy)
    for i in range(blocks):
        for flip, out in enumerate((mine, other)):
            copies[2 * i + flip].wait()
            at = slice(i * rows, (i + 1) * rows)
            out[at] = held[flip, at].astype(jnp.float32).astype(out.dtype)


def pinned(x):
    return pltpu.with_memory_space_constraint(x, pltpu.VMEM)


def unpinned(x):
    return pltpu.with_memory_space_constraint(x, pltpu.HBM)


VMEM_SPEC = pl.BlockSpec(memory_space=pltpu.VMEM)


def call(kernel, name, scalars, operands, outs, scratch, flops):
    return pl.pallas_call(
        kernel,
        out_shape=[pltpu.VMEM(shape, dtype) for shape, dtype in outs],
        grid_spec=pltpu.PrefetchScalarGridSpec(
            num_scalar_prefetch=len(scalars),
            grid=(1,),
            in_specs=[VMEM_SPEC] * len(operands),
            out_specs=[VMEM_SPEC] * len(outs),
            scratch_shapes=scratch,
        ),
        compiler_params=pltpu.CompilerParams(vmem_limit_bytes=VMEM_BYTES),
        cost_estimate=pl.CostEstimate(flops=flops, bytes_accessed=10**6, transcendentals=0),
        name=name,
    )(*scalars, *(pinned(x) for x in operands))


def windows(place, anchors, slowness_codes, rows_x, rows_y):
    blocks = 4
    return pl.pallas_call(
        functools.partial(window_kernel, blocks=blocks),
        out_shape=[
            pltpu.VMEM((rows_x, rows_y), jnp.bfloat16),
            pltpu.HBM((rows_x, rows_y), jnp.bfloat16),
        ],
        grid_spec=pltpu.PrefetchScalarGridSpec(
            num_scalar_prefetch=2,
            grid=(1,),
            in_specs=[pl.BlockSpec(memory_space=pl.ANY)],
            out_specs=[VMEM_SPEC, VMEM_SPEC],
            scratch_shapes=[
                pltpu.VMEM((2, rows_x, rows_y), jnp.int32),
                pltpu.SemaphoreType.DMA((2, blocks)),
            ],
        ),
        compiler_params=pltpu.CompilerParams(vmem_limit_bytes=VMEM_BYTES),
        name="windows",
    )(place, anchors, unpinned(slowness_codes))


def shards(source_top, receiver_top, slowness_codes, slowness_table, anchors):
    shots, _, _, rows_x, rows_y = source_top.shape
    freq_count = lax.axis_size("freq")
    depth_count = lax.axis_size("depth")
    strips = freq_count // 2
    width = rows_x // freq_count
    height = width + 2 * HALO
    lags = 2 * LAG + 1
    tiles = rows_y // LANES
    groups = [(0, tiles // 2), (tiles // 2, tiles)]
    factor = 1.0 / math.sqrt(2.0 * shots * freq_count)
    depth_index = lax.axis_index("depth")
    freq_index = lax.axis_index("freq")
    my_core = depth_index % shots
    group = depth_index // shots
    bf16, f32 = jnp.bfloat16, jnp.float32

    def number(group_at, core_at, strip_at, parity_at):
        return (group_at * shots + core_at) * freq_count + strip_at * 2 + parity_at

    def pairs(move, core):
        found = []
        for g in range(depth_count // shots):
            for c in range(shots):
                for z in range(strips):
                    for x in range(2):
                        to = move(g, c, z, x)
                        if core in (None, c) and to is not None:
                            found.append((number(g, c, z, x), number(*to)))
        return found

    def send(value, move, core=None):
        return lax.ppermute(value, AXES, pairs(move, core))

    def to_core(g, c, z, x):
        return (g, 1 - c, z, x)

    def to_same(g, c, z, x):
        return (g, c, z, 1 - x)

    def to_cross(g, c, z, x):
        return (g, 1 - c, z, 1 - x)

    def up(g, c, z, x):
        return (1, c, z, x) if g == 0 else None

    ring = [0] + list(range(1, strips, 2)) + list(range(2, strips, 2))[::-1]
    spots = {z: p for p, z in enumerate(ring)}

    def onward(g, c, z, x):
        return (g, c, ring[(spots[z] + 1) % strips], x)

    my_strip = freq_index // 2
    spot = jnp.where(
        my_strip == 0,
        0,
        jnp.where(my_strip % 2 == 1, (my_strip + 1) // 2, strips - my_strip // 2),
    )
    place = jnp.stack([group, my_core, freq_index % 2, spot]).astype(jnp.int32)
    angular = (math.pi * (0.45 + 0.5 * (freq_index.astype(f32) + 0.5) / freq_count))[None]
    scalars = (place, angular)

    mine, other = windows(place, anchors, slowness_codes, rows_x, rows_y)
    from_core = send(other, to_core)
    near = (mine, from_core)
    far_first = (send(mine, up, 0), send(from_core, up, 1))

    levels = jnp.pad(slowness_table, (0, LANES - slowness_table.shape[0]))[None]
    tables = []
    for length in (rows_x,) if rows_x == rows_y else (rows_x, rows_y):
        left = residue_tables(length)
        tables += [jnp.asarray(left), jnp.asarray(np.swapaxes(left, 1, 2))]
    wave_x = jnp.asarray(wavenumbers_squared(rows_x)[:, None])
    wave_y = jnp.asarray(wavenumbers_squared(rows_y)[None])
    whole = (4, rows_x, rows_y)
    phase_shape = (2, wave_x.shape[0], wave_y.shape[1])
    index_scratch = pltpu.VMEM((rows_x, rows_y), jnp.int32)
    top_spec = pl.BlockSpec(
        (1, 1, 2, rows_x, rows_y), lambda i, place, angular: (place[1], 0, 0, 0, 0)
    )
    prepared = pl.pallas_call(
        functools.partial(prepare_kernel, shots=shots),
        out_shape=[
            pltpu.VMEM(whole, bf16),
            pltpu.VMEM(whole, bf16),
            pltpu.VMEM((8, LANES), f32),
            pltpu.VMEM((shots, *phase_shape), f32),
            *(pltpu.VMEM(t.shape, t.dtype) for t in tables),
            pltpu.VMEM((shots, rows_x, rows_y), jnp.int32),
        ],
        grid_spec=pltpu.PrefetchScalarGridSpec(
            num_scalar_prefetch=2,
            grid=(1,),
            in_specs=[top_spec] * 2 + [VMEM_SPEC] * (5 + len(tables)),
            out_specs=[VMEM_SPEC] * (5 + len(tables)),
        ),
        compiler_params=pltpu.CompilerParams(vmem_limit_bytes=VMEM_BYTES),
        cost_estimate=pl.CostEstimate(flops=4 * 10**9, bytes_accessed=10**6, transcendentals=0),
        name="prepare",
    )(
        *scalars, unpinned(source_top), unpinned(receiver_top), pinned(mine), pinned(from_core),
        levels, *(unpinned(t) for t in tables), wave_x, wave_y,
    )
    top, first, means, phases, *tables, indices = prepared
    tables = list(tables) if len(tables) == 4 else list(tables) * 2

    far_means = send(means, up)
    mine_later, from_core_later, _ = lax.optimization_barrier((mine, from_core, means))
    far_second = (send(mine_later, up, 1), send(from_core_later, up, 0))

    (before,) = call(
        lead_kernel,
        "lead",
        scalars,
        [first, *far_first, far_means, levels, *tables, wave_x, wave_y],
        [(whole, f32)],
        [pltpu.VMEM(whole, bf16), pltpu.VMEM(whole, bf16), index_scratch, pltpu.VMEM(phase_shape, f32)],
        15 * 10**9,
    )
    def strip_shapes(steps):
        return [
            ((4, end - begin, height, LANES), bf16)
            for _ in range(4 * steps)
            for begin, end in groups
        ]

    made = call(
        functools.partial(planes_kernel, shots=shots, strips=strips, width=width, groups=groups),
        "planes",
        scalars,
        [top, before, *far_second, far_means, indices, means, phases, levels, *tables],
        [((4, tiles, rows_x + 2 * HALO, LANES), bf16)] * shots + strip_shapes(1),
        [pltpu.VMEM(whole, bf16), pltpu.VMEM(whole, bf16), index_scratch],
        15 * 10**9,
    )
    padded_planes, first_strips = made[:shots], made[shots:]
    later_strips = call(
        functools.partial(strips_kernel, shots=shots, strips=strips, width=width, groups=groups),
        "strips",
        (place,),
        padded_planes,
        strip_shapes(strips - 1),
        [],
        10**9,
    )

    def fetch(step, g, after=None):
        if step == 0:
            own, same, core, cross = (first_strips[i * len(groups) + g] for i in range(4))
        else:
            own, same, core, cross = (
                later_strips[(i * (strips - 1) + step - 1) * len(groups) + g] for i in range(4)
            )
        if after is not None:
            own, same, core, cross, _ = lax.optimization_barrier((own, same, core, cross, after))
        return [own, send(same, to_same), send(core, to_core), send(cross, to_cross)]

    def correlate(fields, received, count, dtype):
        operands = fields + received
        return pl.pallas_call(
            functools.partial(
                correlate_kernel, width=width, tiles=count, partial=bool(received)
            ),
            out_shape=pltpu.VMEM((lags, count, width, LANES), dtype),
            grid=(1,),
            in_specs=[VMEM_SPEC] * len(operands),
            out_specs=VMEM_SPEC,
            scratch_shapes=[pltpu.VMEM((16, height, LANES), f32)],
            compiler_params=pltpu.CompilerParams(vmem_limit_bytes=8 * 2**20),
            cost_estimate=pl.CostEstimate(flops=10**9, bytes_accessed=10**6, transcendentals=0),
            name="correlate",
        )(*(pinned(x) for x in operands))

    def finish(own, received, begin, end, image):
        count = end - begin
        operands = [pinned(own), pinned(received)]
        in_specs = [VMEM_SPEC] * 2
        aliases = {}
        if image is not None:
            operands.append(image)
            in_specs.append(pl.BlockSpec(memory_space=pl.ANY))
            aliases = {2: 0}
        return pl.pallas_call(
            functools.partial(finish_kernel, scale=factor),
            out_shape=jax.ShapeDtypeStruct((1, lags, width, rows_y), f32),
            grid=(1,),
            in_specs=in_specs,
            out_specs=pl.BlockSpec(
                (1, lags, width, count * LANES), lambda i: (0, 0, 0, begin // count)
            ),
            input_output_aliases=aliases,
            compiler_params=pltpu.CompilerParams(vmem_limit_bytes=8 * 2**20),
            cost_estimate=pl.CostEstimate(flops=10**9, bytes_accessed=10**6, transcendentals=0),
            name="finish",
        )(*operands)

    image = None
    received = [[] for _ in groups]
    for step in range(strips - 1):
        for g, (begin, end) in enumerate(groups):
            result = correlate(fetch(step, g), received[g], end - begin, bf16)
            received[g] = [send(result, onward)]
    for g, (begin, end) in enumerate(groups):
        own = correlate(fetch(strips - 1, g, result), [], end - begin, f32)
        image = finish(own, received[g][0], begin, end, image)
    return image


def solution(mesh):
    return jax.shard_map(
        shards,
        mesh=mesh,
        in_specs=(
            P(None, "freq", None, None, None),
            P(None, "freq", None, None, None),
            P("depth", None, None),
            P(),
            P(),
        ),
        out_specs=P("depth", None, "freq", None),
        check_vma=False,
    )
```
